128 devices in a mesh: leaf: 8 (over y, core), front: 16 (over x, z).
Axes of the slice: x: 4, y: 4, z: 4, core: 2. Of those that a mesh axis runs over, the one named last changes fastest.
Arguments:
- inv_factors: bfloat16 [8, 2, 1024, 1024], P('leaf', None, 'front')
- panel_rows: bfloat16 [8, 1024, 1024], P('leaf', 'front'), may hold values from -6 to 6
- border: bfloat16 [8, 2048, 2048], P('leaf', 'front'), may hold values from -6 to 6
- tail: bfloat16 [8, 2048, 2048], P('leaf', 'front'), may hold values from -6 to 6
- front_sizes: int32 [8], replicated, may hold values from 1024 to 2048, as said below
- block_map: int32 [8, 16], replicated, may hold values from 0 to 31, as said below
- block_owner: int32 [8, 32], replicated, may hold values from 0 to 47, as said below
Outputs:
- link_factor: bfloat16 [8, 1024, 1024], P('leaf', 'front')
- border_factor: bfloat16 [8, 2048, 2048], P('leaf', 'front')
- parent_update: float32 [8, 4096, 6144], P('leaf', None, 'front')
The draws below stay inside these ranges and needn't reach their ends.
Inputs may be any that keep to these rules, and one draw needn't show every extreme that they name: `front_sizes`: the live rows of some child always equal 2048; every child has at least 1024. `block_map`: the entries of one child's row are distinct. `block_owner`: the entries of one parent's row are distinct; slot s belongs to front index s // 3, so no front index owns more than 3 blocks of a parent, and in every parent's row one front index owns exactly 3.
All inputs are finite; a program needn't handle non-finite values.
Results may differ from the reference program's by a relative error of at most 0.0055.
Values may be sent and summed in bfloat16 or wider, within the bound.
No kernel may reach another device: no remote copies, remote signals or barrier semaphores. Data moves between devices by JAX's collectives and lax.ppermute only.
A program may use at most 64 MiB of HBM per device.

```python
import jax
import jax.numpy as jnp
from jax import lax

PANEL = 1024
BLOCK = 128
SLOTS = 3
CONTRIB = 2048
N_LEAF = 8
N_FRONT = 16


def draw_inv_factors(key, part):
    key = jax.random.fold_in(key, 11)
    diag_key, off_key = jax.random.split(key)
    diagonal = jax.random.uniform(diag_key, (N_LEAF, 2, PANEL), jnp.float32, 0.08, 0.16)
    offdiag = 0.004 * jax.random.normal(off_key, (N_LEAF, 2, PANEL, PANEL), jnp.float32)
    rows_iota = jnp.arange(PANEL)[:, None]
    cols_iota = jnp.arange(PANEL)[None, :]
    lower = jnp.where(rows_iota > cols_iota, offdiag, jnp.float32(0.0))
    eye_part = jnp.where(rows_iota == cols_iota, diagonal[..., None], jnp.float32(0.0))
    return (lower + eye_part).astype(jnp.bfloat16)


def draw_front_sizes(key, part):
    key = jax.random.fold_in(key, 14)
    size_key, full_key = jax.random.split(key)
    contrib_rows = BLOCK * N_FRONT
    sizes = jax.random.randint(size_key, (N_LEAF,), contrib_rows // 2, contrib_rows + 1)
    chosen = jax.random.randint(full_key, (), 0, N_LEAF)
    return sizes.at[chosen].set(contrib_rows).astype(jnp.int32)


def draw_block_map(key, part):
    key = jax.random.fold_in(key, 12)
    keys = jax.random.split(key, N_LEAF)
    return jax.vmap(lambda single: jax.random.permutation(single, 2 * N_FRONT)[:N_FRONT])(keys).astype(jnp.int32)


def owner_row(single):
    total_slots = N_FRONT * SLOTS
    parent_blocks = 2 * N_FRONT
    perm_key, order_key = jax.random.split(single)
    shuffled = jax.random.permutation(perm_key, total_slots).astype(jnp.int32)
    heavy = shuffled[0] // SLOTS
    flags = jnp.where(shuffled // SLOTS == heavy, 1, 0).astype(jnp.int32)
    ranked = jnp.argsort(flags, stable=True)
    others = shuffled[ranked]
    chosen = jnp.concatenate([heavy * SLOTS + jnp.arange(SLOTS, dtype=jnp.int32), others[:parent_blocks - SLOTS]])
    return chosen[jax.random.permutation(order_key, parent_blocks)]


def draw_block_owner(key, part):
    key = jax.random.fold_in(key, 13)
    keys = jax.random.split(key, N_LEAF)
    return jax.vmap(owner_row)(keys).astype(jnp.int32)


def block_scale(rng, shape, cuts, low, high):
    factor_of, own = 1.0, jax.random.fold_in(rng, 6)
    for axis_at, blocks in cuts:
        heights = jnp.exp(jax.random.uniform(jax.random.fold_in(own, axis_at), (blocks,), jnp.float32, low / len(cuts), high / len(cuts)))
        factor_of = factor_of * jnp.repeat(heights, shape[axis_at] // blocks).reshape([-1 if axis == axis_at else 1 for axis in range(len(shape))])
    return factor_of


def bell_draw(own_key, shape, width, most, shards=(), kind=jnp.bfloat16):
    level = block_scale(own_key, shape, shards, -0.22, 0.18) if shards else 1.0
    entries = jax.random.normal(own_key, shape, jnp.float32) * width * level
    return jnp.minimum(jnp.maximum(entries, -most), most).astype(kind)


def setup_inputs(seed: int = 0) -> dict:
    arg_keys = jax.random.split(jax.random.key(seed), 8)
    inv_factors = draw_inv_factors(jax.random.fold_in(arg_keys[7], 71), 0)
    panel_rows = bell_draw(arg_keys[1], (N_LEAF, PANEL, PANEL), 1.0, 6.0, ((0, 8), (1, 16)))
    border = bell_draw(arg_keys[2], (N_LEAF, CONTRIB, 2 * PANEL), 1.0, 6.0, ((0, 8), (1, 16)))
    tail = bell_draw(arg_keys[3], (N_LEAF, CONTRIB, CONTRIB), 1.0, 6.0, ((0, 8), (1, 16)))
    front_sizes = draw_front_sizes(jax.random.fold_in(arg_keys[7], 71), 0)
    block_map = draw_block_map(jax.random.fold_in(arg_keys[7], 71), 0)
    block_owner = draw_block_owner(jax.random.fold_in(arg_keys[7], 71), 0)
    return dict(inv_factors=inv_factors, panel_rows=panel_rows, border=border, tail=tail, front_sizes=front_sizes, block_map=block_map, block_owner=block_owner)


def dot_rows(left_rows, right_rows):
    return lax.dot_general(left_rows, right_rows, (((1,), (1,)), ((), ())), preferred_element_type=jnp.float32)


def reference(inv_factors, panel_rows, border, tail, front_sizes, block_map, block_owner):
    contrib_rows = BLOCK * N_FRONT
    parent_rows = 2 * contrib_rows
    slot_cols = N_FRONT * SLOTS * BLOCK
    positions = jnp.arange(contrib_rows, dtype=jnp.int32)
    inside = positions % BLOCK
    block_of = positions // BLOCK
    parent_update = jnp.zeros((N_LEAF, parent_rows, slot_cols), jnp.float32)
    link_list = []
    factor_list = []
    for child_index in range(N_LEAF):
        first_inv = inv_factors[child_index, 0]
        second_inv = inv_factors[child_index, 1]
        link = dot_rows(panel_rows[child_index], first_inv).astype(jnp.bfloat16)
        first = dot_rows(border[child_index][:, :PANEL], first_inv).astype(jnp.bfloat16)
        updated = (border[child_index][:, PANEL:].astype(jnp.float32) - dot_rows(first, link)).astype(jnp.bfloat16)
        second = dot_rows(updated, second_inv).astype(jnp.bfloat16)
        factor = jnp.concatenate([first, second], axis=1)
        schur = tail[child_index].astype(jnp.float32) - dot_rows(factor, factor)
        live = front_sizes[child_index]
        keep = (positions[:, None] < live) & (positions[None, :] < live)
        contribution = jnp.where(keep, schur, jnp.float32(0.0)).astype(jnp.bfloat16)
        parent = (child_index + N_LEAF // 2) % N_LEAF
        mapped = block_map[child_index][block_of]
        row_index = (mapped * BLOCK + inside).astype(jnp.int32)
        col_index = (block_owner[parent][mapped] * BLOCK + inside).astype(jnp.int32)
        parent_update = parent_update.at[parent, row_index[:, None], col_index[None, :]].add(contribution.astype(jnp.float32))
        link_list.append(link)
        factor_list.append(factor)
    return jnp.stack(link_list), jnp.stack(factor_list), parent_update
```

```python
import functools

import jax
import jax.numpy as jnp
from jax import lax
from jax.experimental import pallas as pl
from jax.experimental.pallas import tpu as pltpu
from jax.sharding import PartitionSpec as P

PANEL = 1024
BLOCK = 128
SLOTS = 3
SIDE = 4
FRONT = SIDE * SIDE
CONTRIB = BLOCK * FRONT
ROWS = PANEL // FRONT
MIB = 1024 * 1024


def dot_nt(left, right):
    return lax.dot_general(
        left, right, (((1,), (1,)), ((), ())), preferred_element_type=jnp.float32
    )


def shift(value, axis, by):
    dx, dz = (by, 0) if axis == "x" else (0, by)
    pairs = [
        (x * SIDE + z, (x + dx) % SIDE * SIDE + (z + dz) % SIDE)
        for x in range(SIDE)
        for z in range(SIDE)
    ]
    return lax.ppermute(value, "front", pairs)


def to_parent(value):
    groups = lax.axis_size("leaf")
    return lax.ppermute(
        value, "leaf", [(g, (g + groups // 2) % groups) for g in range(groups)]
    )


RING = (0, -1, 1, 2)


def gather_half(own, first_axis, second_axis):
    rows = own.shape[0]
    half = rows // 2
    from_left = shift(own, first_axis, 1)
    from_right = shift(own, first_axis, -1)
    far_top = shift(from_left[:half], first_axis, 1)
    far_bottom = shift(from_right[half:], first_axis, -1)
    bundle = jnp.concatenate([own, from_left, from_right, far_top, far_bottom], axis=0)
    left_bundle = shift(bundle, second_axis, 1)
    right_bundle = shift(bundle, second_axis, -1)
    far_low = shift(left_bundle[: 2 * rows], second_axis, 1)
    far_high = shift(right_bundle[2 * rows :], second_axis, -1)

    def places(first, second):
        return [(f, second) if first_axis == "x" else (second, f) for f in first]

    return [
        (bundle, places(RING, 0)),
        (left_bundle, places(RING, -1)),
        (right_bundle, places(RING, 1)),
        (far_low, places(RING[:2], 2)),
        (far_high, places(RING[2:], 2)),
    ]


def gather_pieces(top, bottom):
    bundles, layout = [], []
    for half, parts in enumerate((gather_half(top, "x", "z"), gather_half(bottom, "z", "x"))):
        rows = (top, bottom)[half].shape[0]
        for array, places in parts:
            bundles.append(array)
            layout.append([(half, at * rows, dx, dz) for at, (dx, dz) in enumerate(places)])
    return bundles, layout


def place_of(front, dx, dz):
    x, z = front // SIDE, front % SIDE
    return lax.rem(x + dx + SIDE, SIDE) * SIDE + lax.rem(z + dz + SIDE, SIDE)


def panel_kernel(layout, info, border, *refs):
    count = len(layout)
    bundles = refs[:count]
    link_out, factor_out = refs[count : count + 2]
    mats, link, updated, sems = refs[count + 2 :]
    front = info[1]
    part = ROWS // 2
    copies = [[], [], []]
    for bundle, places in zip(bundles, layout, strict=True):
        for half, at, dx, dz in places:
            row = pl.multiple_of(place_of(front, dx, dz) * ROWS + half * part, part)
            for which in (0, 2, 1):
                copy = pltpu.make_async_copy(
                    bundle.at[pl.ds(at + which * part, part), :],
                    mats.at[which, pl.ds(row, part), :],
                    sems.at[which, len(copies[which])],
                )
                copies[which].append(copy)
    for which in (0, 2, 1):
        for copy in copies[which]:
            copy.start()
    for copy in copies[0]:
        copy.wait()
    wide = 256
    for at in range(0, PANEL, wide):
        factor_out[:, at : at + wide] = dot_nt(
            border[:, :PANEL], mats[0, at : at + wide, :]
        ).astype(jnp.bfloat16)
    for copy in copies[2]:
        copy.wait()

    @pl.loop(0, PANEL // wide)
    def _(step):
        at = pl.multiple_of(step * wide, wide)
        for up in range(0, PANEL, wide):
            link[up : up + wide, pl.ds(at, wide)] = dot_nt(
                mats[2, up : up + wide, :], mats[0, pl.ds(at, wide), :]
            ).astype(jnp.bfloat16)

    link_out[...] = link[pl.ds(pl.multiple_of(front * ROWS, ROWS), ROWS), :]
    for at in range(0, PANEL, wide):
        coupled = dot_nt(factor_out[:, :PANEL], link[at : at + wide, :])
        updated[:, at : at + wide] = (
            border[:, PANEL + at : PANEL + at + wide].astype(jnp.float32) - coupled
        ).astype(jnp.bfloat16)
    for copy in copies[1]:
        copy.wait()
    for at in range(0, PANEL, wide):
        factor_out[:, PANEL + at : PANEL + at + wide] = dot_nt(
            updated[...], mats[1, at : at + wide, :]
        ).astype(jnp.bfloat16)


def eliminate(info, border, bundles, layout):
    blocks = FRONT * 2
    vmem = pl.BlockSpec(memory_space=pltpu.VMEM)
    return pl.pallas_call(
        functools.partial(panel_kernel, layout),
        out_shape=(
            jax.ShapeDtypeStruct((ROWS, PANEL), jnp.bfloat16),
            jax.ShapeDtypeStruct((BLOCK, 2 * PANEL), jnp.bfloat16),
        ),
        in_specs=[pl.BlockSpec(memory_space=pltpu.SMEM), vmem]
        + [pl.BlockSpec(memory_space=pl.ANY)] * len(bundles),
        out_specs=(vmem, vmem),
        scratch_shapes=[
            pltpu.VMEM((3, PANEL, PANEL), jnp.bfloat16),
            pltpu.VMEM((PANEL, PANEL), jnp.bfloat16),
            pltpu.VMEM((BLOCK, PANEL), jnp.bfloat16),
            pltpu.SemaphoreType.DMA((3, blocks)),
        ],
        compiler_params=pltpu.CompilerParams(vmem_limit_bytes=24 * MIB),
        cost_estimate=pl.CostEstimate(
            flops=2 * PANEL**3 + 6 * BLOCK * PANEL**2,
            bytes_accessed=8 * MIB,
            transcendentals=0,
        ),
        name="panels",
    )(info, border, *bundles)


def pack_kernel(info, block_map, block_owner, tail, out):
    parent, child = info[0], info[2]
    for block in range(FRONT):
        slot = block_owner[parent, block_map[child, block]]
        out[slot // SLOTS, lax.rem(slot, SLOTS)] = tail[:, block * BLOCK : (block + 1) * BLOCK]


def pack_tiles(info, block_map, block_owner, tail):
    smem = pl.BlockSpec(memory_space=pltpu.SMEM)
    vmem = pl.BlockSpec(memory_space=pltpu.VMEM)
    return pl.pallas_call(
        pack_kernel,
        out_shape=jax.ShapeDtypeStruct((FRONT, SLOTS, BLOCK, BLOCK), jnp.bfloat16),
        in_specs=[smem, smem, smem, vmem],
        out_specs=vmem,
        compiler_params=pltpu.CompilerParams(vmem_limit_bytes=8 * MIB),
        name="pack",
    )(info, block_map, block_owner, tail)


def update_kernel(layout, info, sizes, block_map, block_owner, tiles, *refs):
    count = len(layout)
    bundles = refs[:count]
    out = refs[count]
    factor, chosen, staged, blank, taken, column, load_sems, store_sems, blank_sem = refs[
        count + 1 :
    ]
    parent, front, child = info[0], info[1], info[2]
    live = sizes[child]
    part = BLOCK // 2
    loads = []
    for bundle, places in zip(bundles, layout, strict=True):
        for half, at, dx, dz in places:
            row = pl.multiple_of(place_of(front, dx, dz) * BLOCK + half * part, part)
            copy = pltpu.make_async_copy(
                bundle.at[pl.ds(at, part), :],
                factor.at[pl.ds(row, part), :],
                load_sems.at[len(loads)],
            )
            copy.start()
            loads.append(copy)
    blank[...] = jnp.zeros_like(blank)
    for slot in range(SLOTS):
        column[slot] = -1

    @pl.loop(0, 2 * FRONT)
    def _(block):
        taken[block] = 0

    @pl.loop(0, FRONT)
    def _(block):
        into = block_map[child, block]
        taken[into] = 1
        slot = block_owner[parent, into]

        @pl.when(slot // SLOTS == front)
        def _():
            column[lax.rem(slot, SLOTS)] = block

    def blank_copy(block):
        row = pl.multiple_of(block * BLOCK, BLOCK)
        return pltpu.make_async_copy(blank, out.at[pl.ds(row, BLOCK), :], blank_sem)

    @pl.loop(0, 2 * FRONT)
    def _(block):
        @pl.when(taken[block] == 0)
        def _():
            blank_copy(block).start()

    for copy in loads:
        copy.wait()
    for slot in range(SLOTS):
        row = pl.multiple_of(jnp.maximum(column[slot], 0) * BLOCK, BLOCK)
        chosen[slot * BLOCK : (slot + 1) * BLOCK, :] = factor[pl.ds(row, BLOCK), :]

    def store(block):
        row = pl.multiple_of(block_map[child, block] * BLOCK, BLOCK)
        return pltpu.make_async_copy(
            staged.at[block], out.at[pl.ds(row, BLOCK), :], store_sems.at[block]
        )

    lane = lax.broadcasted_iota(jnp.int32, (BLOCK, BLOCK), 1)
    line = lax.broadcasted_iota(jnp.int32, (BLOCK, BLOCK), 0)

    @pl.loop(0, FRONT // 2)
    def _(pair):
        top = pl.multiple_of(pair * 2 * BLOCK, 2 * BLOCK)
        product = dot_nt(factor[pl.ds(top, 2 * BLOCK), :], chosen[...])
        for low in range(2):
            block = pair * 2 + low
            for slot in range(SLOTS):
                first = column[slot]
                keep = (
                    (line + block * BLOCK < live)
                    & (lane + first * BLOCK < live)
                    & (lane * 0 + first >= 0)
                )
                schur = (
                    tiles[block, slot].astype(jnp.float32)
                    - product[low * BLOCK : (low + 1) * BLOCK, slot * BLOCK : (slot + 1) * BLOCK]
                )
                staged[block, :, slot * BLOCK : (slot + 1) * BLOCK] = (
                    jnp.where(keep, schur, 0.0).astype(jnp.bfloat16).astype(jnp.float32)
                )
            store(block).start()

    for block in range(FRONT):
        store(block).wait()

    @pl.loop(0, FRONT)
    def _(block):
        blank_copy(0).wait()


def update_parent(info, sizes, block_map, block_owner, tiles, bundles, layout):
    smem = pl.BlockSpec(memory_space=pltpu.SMEM)
    vmem = pl.BlockSpec(memory_space=pltpu.VMEM)
    held = pl.BlockSpec(memory_space=pl.ANY)
    return pl.pallas_call(
        functools.partial(update_kernel, layout),
        out_shape=jax.ShapeDtypeStruct((2 * CONTRIB, SLOTS * BLOCK), jnp.float32),
        in_specs=[smem, smem, smem, smem, vmem] + [held] * len(bundles),
        out_specs=held,
        scratch_shapes=[
            pltpu.VMEM((CONTRIB, 2 * PANEL), jnp.bfloat16),
            pltpu.VMEM((SLOTS * BLOCK, 2 * PANEL), jnp.bfloat16),
            pltpu.VMEM((FRONT, BLOCK, SLOTS * BLOCK), jnp.float32),
            pltpu.VMEM((BLOCK, SLOTS * BLOCK), jnp.float32),
            pltpu.SMEM((2 * FRONT,), jnp.int32),
            pltpu.SMEM((SLOTS,), jnp.int32),
            pltpu.SemaphoreType.DMA((2 * FRONT,)),
            pltpu.SemaphoreType.DMA((FRONT,)),
            pltpu.SemaphoreType.DMA,
        ],
        compiler_params=pltpu.CompilerParams(vmem_limit_bytes=32 * MIB),
        cost_estimate=pl.CostEstimate(
            flops=2 * CONTRIB * SLOTS * BLOCK * 2 * PANEL,
            bytes_accessed=16 * MIB,
            transcendentals=0,
        ),
        name="update",
    )(info, sizes, block_map, block_owner, tiles, *bundles)


def per_device(inv_factors, panel_rows, border, tail, front_sizes, block_map, block_owner):
    groups = lax.axis_size("leaf")
    group = lax.axis_index("leaf")
    front = lax.axis_index("front")
    info = jnp.stack([group, front, (group + groups // 2) % groups]).astype(jnp.int32)

    tail_here = to_parent(tail[0])
    packed = pack_tiles(info, block_map, block_owner, tail_here)
    tiles = lax.all_to_all(packed, "front", split_axis=0, concat_axis=0, tiled=True)

    part = ROWS // 2
    own = jnp.concatenate([inv_factors[0], panel_rows], axis=0)
    top = own[:, :part].reshape(3 * part, PANEL)
    bottom = own[:, part:].reshape(3 * part, PANEL)
    bundles, layout = gather_pieces(top, bottom)
    link_local, factor_local = eliminate(info, border[0], bundles, layout)

    child_rows = to_parent(factor_local)
    bundles, layout = gather_pieces(child_rows[: BLOCK // 2], child_rows[BLOCK // 2 :])
    update = update_parent(info, front_sizes, block_map, block_owner, tiles, bundles, layout)
    return link_local[None], factor_local[None], update[None]


def solution(mesh):
    return jax.shard_map(
        per_device,
        mesh=mesh,
        in_specs=(
            P("leaf", None, "front", None),
            P("leaf", "front", None),
            P("leaf", "front", None),
            P("leaf", "front", None),
            P(),
            P(),
            P(),
        ),
        out_specs=(P("leaf", "front", None), P("leaf", "front", None), P("leaf", None, "front")),
        check_vma=False,
    )
```

```python
import functools

import jax
import jax.numpy as jnp
from jax import lax
from jax.experimental import pallas as pl
from jax.experimental.pallas import tpu as pltpu
from jax.sharding import PartitionSpec as P

PANEL = 1024
BLOCK = 128
SLOTS = 3
SIDE = 4
FRONT = SIDE * SIDE
CONTRIB = BLOCK * FRONT
ROWS = PANEL // FRONT
MIB = 1024 * 1024


def dot_nt(left, right):
    return lax.dot_general(
        left, right, (((1,), (1,)), ((), ())), preferred_element_type=jnp.float32
    )


def shift(value, axis, by):
    dx, dz = (by, 0) if axis == "x" else (0, by)
    pairs = [
        (x * SIDE + z, (x + dx) % SIDE * SIDE + (z + dz) % SIDE)
        for x in range(SIDE)
        for z in range(SIDE)
    ]
    return lax.ppermute(value, "front", pairs)


def to_parent(value):
    groups = lax.axis_size("leaf")
    return lax.ppermute(
        value, "leaf", [(g, (g + groups // 2) % groups) for g in range(groups)]
    )


RING = (0, -1, 1, 2)


def bundle_of(own, axis):
    half = own.shape[0] // 2
    from_left = shift(own, axis, 1)
    from_right = shift(own, axis, -1)
    far_top = shift(from_left[:half], axis, 1)
    far_bottom = shift(from_right[half:], axis, -1)
    return jnp.concatenate([own, from_left, from_right, far_top, far_bottom], axis=0)


def spread(bundle, axis):
    half = bundle.shape[0] // 2
    left = shift(bundle, axis, 1)
    right = shift(bundle, axis, -1)
    far_low = shift(left[:half], axis, 1)
    far_high = shift(right[half:], axis, -1)
    return [bundle, left, right, far_low, far_high]


def places(x_first):
    found = []
    for part, second in ((RING, 0), (RING, -1), (RING, 1), (RING[:2], 2), (RING[2:], 2)):
        found.append([(first, second) if x_first else (second, first) for first in part])
    return found


X_FIRST, Z_FIRST = places(True), places(False)


def place_of(front, dx, dz):
    x, z = front // SIDE, front % SIDE
    return lax.rem(x + dx + SIDE, SIDE) * SIDE + lax.rem(z + dz + SIDE, SIDE)


def family():
    groups = lax.axis_size("leaf")
    parent = lax.axis_index("leaf")
    return parent, lax.rem(parent + groups // 2, groups), lax.axis_index("front")


def unpack(front, bundles, which, mat):
    part = ROWS // 2
    for half, layout in enumerate((X_FIRST, Z_FIRST)):
        for bundle, blocks in zip(bundles[half * 5 : half * 5 + 5], layout, strict=True):
            for at, (dx, dz) in enumerate(blocks):
                row = pl.multiple_of(place_of(front, dx, dz) * ROWS + half * part, part)
                top = (at * 3 + which) * part
                mat[pl.ds(row, part), :] = bundle[top : top + part, :]


WIDE = 256


def project(rows, inverse, keep):
    for at in range(0, PANEL, WIDE):
        upto = at + WIDE
        keep(at, dot_nt(rows[:, :upto], inverse[at:upto, :upto]))


def first_kernel(border, *refs):
    bundles, (first, inverse) = refs[:10], refs[10:]
    unpack(lax.axis_index("front"), bundles, 0, inverse)

    def keep(at, value):
        first[:, at : at + WIDE] = value.astype(jnp.bfloat16)

    project(border, inverse, keep)


def second_kernel(border, first, *refs):
    bundles, (link_out, factor) = refs[:10], refs[10:12]
    mats, link, updated = refs[12:]
    front = lax.axis_index("front")
    for which in range(3):
        unpack(front, bundles, which, mats.at[which])
    factor[:, :PANEL] = first[...]

    def keep_link(at, value):
        link[:, at : at + WIDE] = value.astype(jnp.bfloat16)

    def keep_second(at, value):
        factor[:, PANEL + at : PANEL + at + WIDE] = value.astype(jnp.bfloat16)

    project(mats.at[2], mats.at[0], keep_link)
    link_out[...] = link[pl.ds(pl.multiple_of(front * ROWS, ROWS), ROWS), :]
    for at in range(0, PANEL, WIDE):
        coupled = dot_nt(first[...], link[at : at + WIDE, :])
        updated[:, at : at + WIDE] = (
            border[:, PANEL + at : PANEL + at + WIDE].astype(jnp.float32) - coupled
        ).astype(jnp.bfloat16)
    project(updated, mats.at[1], keep_second)


VMEM_SPEC = pl.BlockSpec(memory_space=pltpu.VMEM)
SMEM_SPEC = pl.BlockSpec(memory_space=pltpu.SMEM)


def first_columns(border, bundles):
    return pl.pallas_call(
        first_kernel,
        out_shape=jax.ShapeDtypeStruct((BLOCK, PANEL), jnp.bfloat16),
        in_specs=[VMEM_SPEC] * 11,
        out_specs=VMEM_SPEC,
        scratch_shapes=[pltpu.VMEM((PANEL, PANEL), jnp.bfloat16)],
        compiler_params=pltpu.CompilerParams(vmem_limit_bytes=8 * MIB),
        cost_estimate=pl.CostEstimate(
            flops=2 * BLOCK * PANEL**2, bytes_accessed=3 * MIB, transcendentals=0
        ),
        name="first",
    )(border, *bundles)


def second_columns(border, first, bundles):
    return pl.pallas_call(
        second_kernel,
        out_shape=(
            jax.ShapeDtypeStruct((ROWS, PANEL), jnp.bfloat16),
            jax.ShapeDtypeStruct((BLOCK, 2 * PANEL), jnp.bfloat16),
        ),
        in_specs=[VMEM_SPEC] * 12,
        out_specs=(VMEM_SPEC,) * 2,
        scratch_shapes=[
            pltpu.VMEM((3, PANEL, PANEL), jnp.bfloat16),
            pltpu.VMEM((PANEL, PANEL), jnp.bfloat16),
            pltpu.VMEM((BLOCK, PANEL), jnp.bfloat16),
        ],
        compiler_params=pltpu.CompilerParams(vmem_limit_bytes=16 * MIB),
        cost_estimate=pl.CostEstimate(
            flops=2 * PANEL**3 + 4 * BLOCK * PANEL**2,
            bytes_accessed=8 * MIB,
            transcendentals=0,
        ),
        name="second",
    )(border, first, *bundles)


def tail_kernel(tail, *outs):
    z = lax.rem(lax.axis_index("front"), SIDE)
    for step, out in enumerate(outs):
        to = lax.rem(z + step, SIDE)
        for x in range(SIDE):
            at = pl.multiple_of((x * SIDE + to) * BLOCK, BLOCK)
            out[:, x * BLOCK : (x + 1) * BLOCK] = tail[:, pl.ds(at, BLOCK)]


LINE = SIDE * BLOCK


def split_tail(tail):
    return pl.pallas_call(
        tail_kernel,
        out_shape=(jax.ShapeDtypeStruct((BLOCK, LINE), jnp.bfloat16),) * SIDE,
        in_specs=[VMEM_SPEC],
        out_specs=(VMEM_SPEC,) * SIDE,
        compiler_params=pltpu.CompilerParams(vmem_limit_bytes=4 * MIB),
        cost_estimate=pl.CostEstimate(flops=0, bytes_accessed=MIB, transcendentals=0),
        name="tail",
    )(tail)


def tile_kernel(sizes, rows_z, rows_x, *refs):
    tails, outs, (product,) = refs[:SIDE], refs[SIDE : SIDE + 2], refs[SIDE + 2 :]
    front = lax.axis_index("front")
    live = sizes[lax.axis_index("leaf")]
    x, z = front // SIDE, lax.rem(front, SIDE)
    lane = lax.broadcasted_iota(jnp.int32, (BLOCK, BLOCK), 1)
    line = lax.broadcasted_iota(jnp.int32, (BLOCK, BLOCK), 0)
    for at in range(0, LINE, WIDE):
        product[:, at : at + WIDE] = dot_nt(rows_z[...], rows_x[at : at + WIDE, :])
    for up, dz in enumerate(RING):
        row_z = lax.rem(z + dz + SIDE, SIDE)
        for across, dx in enumerate(RING):
            col_x = lax.rem(x + dx + SIDE, SIDE)
            columns = slice(across * BLOCK, (across + 1) * BLOCK)
            keep = (line + (x * SIDE + row_z) * BLOCK < live) & (
                lane + (col_x * SIDE + z) * BLOCK < live
            )
            old = tails[-dz % SIDE][:, pl.ds(pl.multiple_of(col_x * BLOCK, BLOCK), BLOCK)]
            schur = old.astype(jnp.float32) - product[up * BLOCK : (up + 1) * BLOCK, columns]
            value = jnp.where(keep, schur, 0.0).astype(jnp.bfloat16)
            for chunk, out in enumerate(outs):

                @pl.when(row_z // 2 == chunk)
                def _():
                    row = pl.multiple_of(lax.rem(row_z, 2) * BLOCK, BLOCK)
                    out[pl.ds(row, BLOCK), columns] = value


def make_tile(sizes, rows_z, rows_x, tails):
    return pl.pallas_call(
        tile_kernel,
        out_shape=(jax.ShapeDtypeStruct((LINE // 2, LINE), jnp.bfloat16),) * 2,
        in_specs=[SMEM_SPEC] + [VMEM_SPEC] * (2 + SIDE),
        out_specs=(VMEM_SPEC,) * 2,
        scratch_shapes=[pltpu.VMEM((LINE, LINE), jnp.float32)],
        compiler_params=pltpu.CompilerParams(vmem_limit_bytes=8 * MIB),
        cost_estimate=pl.CostEstimate(
            flops=4 * LINE * LINE * PANEL, bytes_accessed=6 * MIB, transcendentals=0
        ),
        name="tile",
    )(sizes, rows_z, rows_x, *tails)


def pack_kernel(block_map, block_owner, line, *outs):
    parent, child, front = family()
    x, z = front // SIDE, lax.rem(front, SIDE)
    rows = LINE // 2
    for up, dz in enumerate(RING):
        for across, dx in enumerate(RING):
            block = place_of(front, dx, dz)
            slot = block_owner[parent, block_map[child, block]]
            owner = slot // SLOTS
            for step, out in enumerate(outs):

                @pl.when(
                    (lax.rem(owner, SIDE) == z)
                    & (lax.rem(owner // SIDE - x + SIDE, SIDE) == step)
                )
                def _():
                    out[lax.rem(slot, SLOTS)] = line[
                        up * rows : (up + 1) * rows, across * BLOCK : (across + 1) * BLOCK
                    ]


def pack_tiles(block_map, block_owner, line):
    shape = jax.ShapeDtypeStruct((SLOTS, LINE // 2, BLOCK), jnp.bfloat16)
    return pl.pallas_call(
        pack_kernel,
        out_shape=(shape,) * SIDE,
        in_specs=[SMEM_SPEC, SMEM_SPEC, VMEM_SPEC],
        out_specs=(VMEM_SPEC,) * SIDE,
        compiler_params=pltpu.CompilerParams(vmem_limit_bytes=4 * MIB),
        cost_estimate=pl.CostEstimate(flops=0, bytes_accessed=2 * MIB, transcendentals=0),
        name="pack",
    )(block_map, block_owner, line)


def blank_kernel(block_map, out, blank, taken, sem):
    _, child, _ = family()
    blank[...] = jnp.zeros_like(blank)

    @pl.loop(0, 2 * FRONT)
    def _(block):
        taken[block] = 0

    @pl.loop(0, FRONT)
    def _(block):
        taken[block_map[child, block]] = 1

    def copy(block):
        row = pl.multiple_of(block * BLOCK, BLOCK)
        return pltpu.make_async_copy(blank, out.at[pl.ds(row, BLOCK), :], sem)

    @pl.loop(0, 2 * FRONT)
    def _(block):
        @pl.when(taken[block] == 0)
        def _():
            copy(block).start()

    @pl.loop(0, FRONT)
    def _(block):
        copy(0).wait()


PARENT = jax.ShapeDtypeStruct((2 * CONTRIB, SLOTS * BLOCK), jnp.float32)
HELD = pl.BlockSpec(memory_space=pl.ANY)


def blank_rows(block_map):
    return pl.pallas_call(
        blank_kernel,
        out_shape=PARENT,
        in_specs=[SMEM_SPEC],
        out_specs=HELD,
        scratch_shapes=[
            pltpu.VMEM((BLOCK, SLOTS * BLOCK), jnp.float32),
            pltpu.SMEM((2 * FRONT,), jnp.int32),
            pltpu.SemaphoreType.DMA,
        ],
        compiler_params=pltpu.CompilerParams(vmem_limit_bytes=2 * MIB),
        cost_estimate=pl.CostEstimate(flops=0, bytes_accessed=3 * MIB, transcendentals=0),
        name="blank",
    )(block_map)


def place_kernel(chunk, block_map, block_owner, *refs):
    tiles, (out, staged, held, sems) = refs[:SIDE], refs[SIDE + 1 :]
    parent, child, front = family()
    for slot in range(SLOTS):
        held[slot] = 0

    @pl.loop(0, FRONT)
    def _(block):
        slot = block_owner[parent, block_map[child, block]]

        @pl.when(slot // SLOTS == front)
        def _():
            held[lax.rem(slot, SLOTS)] = 1

    none = lax.broadcasted_iota(jnp.int32, (BLOCK, BLOCK), 0) * 0
    copies = []
    for step, tile in enumerate(tiles):
        x = lax.rem(front // SIDE - step + SIDE, SIDE)
        for up in range(2):
            block = x * SIDE + chunk * 2 + up
            here = len(copies)
            for slot in range(SLOTS):
                value = tile[slot, up * BLOCK : (up + 1) * BLOCK, :].astype(jnp.float32)
                staged[here, :, slot * BLOCK : (slot + 1) * BLOCK] = jnp.where(
                    none + held[slot] > 0, value, 0.0
                )
            row = pl.multiple_of(block_map[child, block] * BLOCK, BLOCK)
            copy = pltpu.make_async_copy(
                staged.at[here], out.at[pl.ds(row, BLOCK), :], sems.at[here]
            )
            copy.start()
            copies.append(copy)
    for copy in copies:
        copy.wait()


def place_tiles(chunk, block_map, block_owner, tiles, parent_rows):
    return pl.pallas_call(
        functools.partial(place_kernel, chunk),
        out_shape=PARENT,
        in_specs=[SMEM_SPEC] * 2 + [VMEM_SPEC] * SIDE + [HELD],
        out_specs=HELD,
        scratch_shapes=[
            pltpu.VMEM((2 * SIDE, BLOCK, SLOTS * BLOCK), jnp.float32),
            pltpu.SMEM((SLOTS,), jnp.int32),
            pltpu.SemaphoreType.DMA((2 * SIDE,)),
        ],
        input_output_aliases={2 + SIDE: 0},
        compiler_params=pltpu.CompilerParams(vmem_limit_bytes=6 * MIB),
        cost_estimate=pl.CostEstimate(flops=0, bytes_accessed=3 * MIB, transcendentals=0),
        name="place",
    )(block_map, block_owner, *tiles, parent_rows)


def per_device(inv_factors, panel_rows, border, tail, front_sizes, block_map, block_owner):
    tails = split_tail(tail[0])
    tails = [tails[0]] + [shift(tails[step], "z", step) for step in range(1, SIDE)]

    part = ROWS // 2
    own = jnp.concatenate([inv_factors[0], panel_rows], axis=0)
    top = bundle_of(own[:, :part].reshape(3 * part, PANEL), "x")
    bottom = bundle_of(own[:, part:].reshape(3 * part, PANEL), "z")
    bundles = spread(top, "z") + spread(bottom, "x")
    tails, bundles = lax.optimization_barrier((tails, bundles))
    first = first_columns(border[0], bundles)
    link_local, factor_local = second_columns(border[0], first, bundles)

    chunks = make_tile(
        front_sizes, bundle_of(factor_local, "z"), bundle_of(factor_local, "x"), tails
    )

    update = blank_rows(block_map)
    for chunk, rows in enumerate(chunks):
        line = bundle_of(to_parent(rows), "z")
        packed = pack_tiles(block_map, block_owner, line)
        tiles = [packed[0]] + [shift(packed[step], "x", step) for step in range(1, SIDE)]
        update = place_tiles(chunk, block_map, block_owner, tiles, update)
    return link_local[None], factor_local[None], update[None]


def solution(mesh):
    return jax.shard_map(
        per_device,
        mesh=mesh,
        in_specs=(
            P("leaf", None, "front", None),
            P("leaf", "front", None),
            P("leaf", "front", None),
            P("leaf", "front", None),
            P(),
            P(),
            P(),
        ),
        out_specs=(P("leaf", "front", None), P("leaf", "front", None), P("leaf", None, "front")),
        check_vma=False,
    )
```

```python
import functools

import jax
import jax.numpy as jnp
from jax import lax
from jax.experimental import pallas as pl
from jax.experimental.pallas import tpu as pltpu
from jax.sharding import PartitionSpec as P

PANEL = 1024
BLOCK = 128
SLOTS = 3
SIDE = 4
FRONT = SIDE * SIDE
CONTRIB = BLOCK * FRONT
ROWS = PANEL // FRONT
MIB = 1024 * 1024


def dot_nt(left, right):
    return lax.dot_general(
        left, right, (((1,), (1,)), ((), ())), preferred_element_type=jnp.float32
    )


def shift(value, axis, by):
    dx, dz = (by, 0) if axis == "x" else (0, by)
    pairs = [
        (x * SIDE + z, (x + dx) % SIDE * SIDE + (z + dz) % SIDE)
        for x in range(SIDE)
        for z in range(SIDE)
    ]
    return lax.ppermute(value, "front", pairs)


def to_parent(value):
    groups = lax.axis_size("leaf")
    return lax.ppermute(
        value, "leaf", [(g, (g + groups // 2) % groups) for g in range(groups)]
    )


RING = (0, -1, 1, 2)


def bundle_of(own, axis):
    half = own.shape[0] // 2
    from_left = shift(own, axis, 1)
    from_right = shift(own, axis, -1)
    far_top = shift(from_left[:half], axis, 1)
    far_bottom = shift(from_right[half:], axis, -1)
    return jnp.concatenate([own, from_left, from_right, far_top, far_bottom], axis=0)


def spread(bundle, axis):
    half = bundle.shape[0] // 2
    left = shift(bundle, axis, 1)
    right = shift(bundle, axis, -1)
    far_low = shift(left[:half], axis, 1)
    far_high = shift(right[half:], axis, -1)
    return [bundle, left, right, far_low, far_high]


def places(x_first):
    found = []
    for part, second in ((RING, 0), (RING, -1), (RING, 1), (RING[:2], 2), (RING[2:], 2)):
        found.append([(first, second) if x_first else (second, first) for first in part])
    return found


X_FIRST, Z_FIRST = places(True), places(False)


def place_of(front, dx, dz):
    x, z = front // SIDE, front % SIDE
    return lax.rem(x + dx + SIDE, SIDE) * SIDE + lax.rem(z + dz + SIDE, SIDE)


def family():
    groups = lax.axis_size("leaf")
    parent = lax.axis_index("leaf")
    return parent, lax.rem(parent + groups // 2, groups), lax.axis_index("front")


def unpack_inverses(front, bundles, mats):
    z = lax.rem(front, SIDE)
    for bundle, dz, start in zip(bundles, (0, -1, 1, 2, 2), (0, 0, 0, 0, CHUNKS // 2), strict=True):
        place = lax.rem(z + dz + SIDE, SIDE) * ROWS
        for at in range(bundle.shape[0] // (2 * ROWS)):
            x, chunk = LOWER[start + at]
            row = pl.multiple_of(place + x * SIDE * ROWS, ROWS)
            for which in range(2):
                top = (at * 2 + which) * ROWS
                mats[which, pl.ds(row, ROWS), chunk * WIDE : (chunk + 1) * WIDE] = bundle[
                    top : top + ROWS, :
                ]


def unpack_panel(front, bundles, mat):
    for bundle, blocks in zip(bundles, Z_FIRST, strict=True):
        for at, (dx, dz) in enumerate(blocks):
            row = pl.multiple_of(place_of(front, dx, dz) * ROWS, ROWS)
            mat[pl.ds(row, ROWS), :] = bundle[at * ROWS : (at + 1) * ROWS, :]


WIDE = SIDE * ROWS
LOWER = [(x, chunk) for x in range(SIDE) for chunk in range(x + 1)]
CHUNKS = len(LOWER)


def project(rows, inverse, keep):
    for at in range(0, PANEL, WIDE):
        upto = at + WIDE
        keep(at, dot_nt(rows[:, :upto], inverse[at:upto, :upto]))


def lower_kernel(*refs):
    sources, out = refs[:5], refs[5]
    x = lax.axis_index("front") // SIDE
    blocks = [(sources[0], 0, 0), (sources[1], 0, -1), (sources[2], 0, 1)]
    blocks += [(sources[3], 0, 2), (sources[4], 1, 2)]
    for source, first, dx in blocks:
        from_x = lax.rem(x + dx + SIDE, SIDE)
        start = (from_x * (from_x + 1)) // 2
        for chunk in range(SIDE):

            @pl.when(chunk <= from_x)
            def _():
                row = pl.multiple_of((start + chunk) * 2 * ROWS + first * ROWS, ROWS)
                out[pl.ds(row, source.shape[0]), :] = source[:, chunk * WIDE : (chunk + 1) * WIDE]


def lower_chunks(own, left, right, far_first, far_second):
    return pl.pallas_call(
        lower_kernel,
        out_shape=jax.ShapeDtypeStruct((CHUNKS * 2 * ROWS, WIDE), jnp.bfloat16),
        in_specs=[VMEM_SPEC] * 5,
        out_specs=VMEM_SPEC,
        compiler_params=pltpu.CompilerParams(vmem_limit_bytes=4 * MIB),
        cost_estimate=pl.CostEstimate(flops=0, bytes_accessed=MIB, transcendentals=0),
        name="lower",
    )(own, left, right, far_first, far_second)


def panel_kernel(border, *refs):
    inverses, panels, (link_out, factor) = refs[:5], refs[5:10], refs[10:12]
    mats, panel, link, updated = refs[12:]
    front = lax.axis_index("front")
    unpack_inverses(front, inverses, mats)

    def keep_first(at, value):
        factor[:, at : at + WIDE] = value.astype(jnp.bfloat16)

    def keep_link(at, value):
        link[:, at : at + WIDE] = value.astype(jnp.bfloat16)

    def keep_second(at, value):
        factor[:, PANEL + at : PANEL + at + WIDE] = value.astype(jnp.bfloat16)

    project(border, mats.at[0], keep_first)
    unpack_panel(front, panels, panel)
    project(panel, mats.at[0], keep_link)
    link_out[...] = link[pl.ds(pl.multiple_of(front * ROWS, ROWS), ROWS), :]
    for at in range(0, PANEL, WIDE):
        coupled = dot_nt(factor[:, :PANEL], link[at : at + WIDE, :])
        updated[:, at : at + WIDE] = (
            border[:, PANEL + at : PANEL + at + WIDE].astype(jnp.float32) - coupled
        ).astype(jnp.bfloat16)
    project(updated, mats.at[1], keep_second)


VMEM_SPEC = pl.BlockSpec(memory_space=pltpu.VMEM)
SMEM_SPEC = pl.BlockSpec(memory_space=pltpu.SMEM)


def eliminate(border, inverses, panels):
    return pl.pallas_call(
        panel_kernel,
        out_shape=(
            jax.ShapeDtypeStruct((ROWS, PANEL), jnp.bfloat16),
            jax.ShapeDtypeStruct((BLOCK, 2 * PANEL), jnp.bfloat16),
        ),
        in_specs=[VMEM_SPEC] * 11,
        out_specs=(VMEM_SPEC,) * 2,
        scratch_shapes=[
            pltpu.VMEM((2, PANEL, PANEL), jnp.bfloat16),
            pltpu.VMEM((PANEL, PANEL), jnp.bfloat16),
            pltpu.VMEM((PANEL, PANEL), jnp.bfloat16),
            pltpu.VMEM((BLOCK, PANEL), jnp.bfloat16),
        ],
        compiler_params=pltpu.CompilerParams(vmem_limit_bytes=16 * MIB),
        cost_estimate=pl.CostEstimate(
            flops=2 * PANEL**3 + 6 * BLOCK * PANEL**2,
            bytes_accessed=8 * MIB,
            transcendentals=0,
        ),
        name="panels",
    )(border, *inverses, *panels)


LINE = SIDE * BLOCK
CHUNKS_OF_ROWS = ((0, 1), (2, 3))
HALF = ROWS // 2
TAIL_AT, PANEL_AT, ON_AT, MESSAGE = 0, ROWS, 2 * ROWS - HALF, 2 * ROWS + HALF


def message_kernel(tail, panel, up, down, kept):
    z = lax.rem(lax.axis_index("front"), SIDE)

    def columns(step, x):
        at = pl.multiple_of((x * SIDE + lax.rem(z + step, SIDE)) * BLOCK, BLOCK)
        return tail[:, pl.ds(at, BLOCK)]

    for x in range(SIDE):
        here = slice(x * BLOCK, (x + 1) * BLOCK)
        there = slice(LINE + x * BLOCK, LINE + (x + 1) * BLOCK)
        kept[:, here] = columns(0, x)
        for step, out in ((1, up), (SIDE - 1, down)):
            block = columns(step, x)
            out[:ROWS, here] = block[:ROWS]
            out[:ROWS, there] = block[ROWS:]
        block = columns(2, x)
        for part, out in enumerate((up, down)):
            first = part * ROWS
            out[2 * ROWS :, here] = block[first : first + HALF]
            out[2 * ROWS :, there] = block[first + HALF : first + ROWS]
    up[ROWS : ROWS + HALF] = panel[HALF:]
    up[ROWS + HALF : 2 * ROWS] = panel[:HALF]
    down[ROWS : ROWS + HALF] = panel[:HALF]
    down[ROWS + HALF : 2 * ROWS] = panel[HALF:]


def make_messages(tail, panel):
    message = jax.ShapeDtypeStruct((MESSAGE, PANEL), jnp.bfloat16)
    return pl.pallas_call(
        message_kernel,
        out_shape=(message, message, jax.ShapeDtypeStruct((BLOCK, LINE), jnp.bfloat16)),
        in_specs=[VMEM_SPEC] * 2,
        out_specs=(VMEM_SPEC,) * 3,
        compiler_params=pltpu.CompilerParams(vmem_limit_bytes=4 * MIB),
        cost_estimate=pl.CostEstimate(flops=0, bytes_accessed=2 * MIB, transcendentals=0),
        name="messages",
    )(tail, panel)


def tile_kernel(chunk, sizes, rows_z, rows_x, *refs):
    (kept, low, high, far_low, far_high), (out, product, tails, rows) = refs[:5], refs[5:]
    front = lax.axis_index("front")
    live = sizes[lax.axis_index("leaf")]
    x, z = front // SIDE, lax.rem(front, SIDE)
    lane = lax.broadcasted_iota(jnp.int32, (BLOCK, BLOCK), 1)
    line = lax.broadcasted_iota(jnp.int32, (BLOCK, BLOCK), 0)
    tails[0] = kept[...]
    for step, source in ((1, low), (SIDE - 1, high)):
        tails[step, :ROWS] = source[:ROWS, :LINE]
        tails[step, ROWS:] = source[:ROWS, LINE:]
    for part, source in enumerate((far_low, far_high)):
        first = part * ROWS
        tails[2, first : first + HALF] = source[HALF:, :LINE]
        tails[2, first + HALF : first + ROWS] = source[HALF:, LINE:]
    for up, row_z in enumerate(chunk):
        away = lax.rem(row_z - z + SIDE, SIDE)
        at = jnp.where(away == 0, 0, jnp.where(away == SIDE - 1, 1, away + 1))
        at = pl.multiple_of(at * BLOCK, BLOCK)
        rows[up * BLOCK : (up + 1) * BLOCK, :] = rows_z[pl.ds(at, BLOCK), :]
    for at in range(0, LINE, WIDE):
        product[:, at : at + WIDE] = dot_nt(rows[...], rows_x[at : at + WIDE, :])
    for up, row_z in enumerate(chunk):
        step = lax.rem(z - row_z + SIDE, SIDE)
        for across, dx in enumerate(RING):
            col_x = lax.rem(x + dx + SIDE, SIDE)
            columns = slice(across * BLOCK, (across + 1) * BLOCK)
            keep = (line + (x * SIDE + row_z) * BLOCK < live) & (
                lane + (col_x * SIDE + z) * BLOCK < live
            )
            old = tails[step, :, pl.ds(pl.multiple_of(col_x * BLOCK, BLOCK), BLOCK)]
            schur = old.astype(jnp.float32) - product[up * BLOCK : (up + 1) * BLOCK, columns]
            out[up * BLOCK : (up + 1) * BLOCK, columns] = jnp.where(keep, schur, 0.0).astype(
                jnp.bfloat16
            )


def make_tile(chunk, sizes, rows_z, rows_x, tails):
    rows = len(chunk) * BLOCK
    return pl.pallas_call(
        functools.partial(tile_kernel, chunk),
        out_shape=jax.ShapeDtypeStruct((rows, LINE), jnp.bfloat16),
        in_specs=[SMEM_SPEC] + [VMEM_SPEC] * 7,
        out_specs=VMEM_SPEC,
        scratch_shapes=[
            pltpu.VMEM((rows, LINE), jnp.float32),
            pltpu.VMEM((SIDE, BLOCK, LINE), jnp.bfloat16),
            pltpu.VMEM((rows, 2 * PANEL), jnp.bfloat16),
        ],
        compiler_params=pltpu.CompilerParams(vmem_limit_bytes=8 * MIB),
        cost_estimate=pl.CostEstimate(
            flops=4 * rows * LINE * PANEL, bytes_accessed=5 * MIB, transcendentals=0
        ),
        name="tile",
    )(sizes, rows_z, rows_x, *tails)


def pack_kernel(block_map, block_owner, line, out):
    parent, child, front = family()
    x, z = front // SIDE, lax.rem(front, SIDE)
    rows = line.shape[0] // SIDE
    for up, dz in enumerate(RING):
        for across, dx in enumerate(RING):
            block = place_of(front, dx, dz)
            slot = block_owner[parent, block_map[child, block]]
            owner = slot // SLOTS

            @pl.when(lax.rem(owner, SIDE) == z)
            def _():
                step = lax.rem(owner // SIDE - x + SIDE, SIDE)
                out[step, lax.rem(slot, SLOTS)] = line[
                    up * rows : (up + 1) * rows, across * BLOCK : (across + 1) * BLOCK
                ]


def pack_tiles(block_map, block_owner, line):
    return pl.pallas_call(
        pack_kernel,
        out_shape=jax.ShapeDtypeStruct(
            (SIDE, SLOTS, line.shape[0] // SIDE, BLOCK), jnp.bfloat16
        ),
        in_specs=[SMEM_SPEC, SMEM_SPEC, VMEM_SPEC],
        out_specs=VMEM_SPEC,
        compiler_params=pltpu.CompilerParams(vmem_limit_bytes=4 * MIB),
        cost_estimate=pl.CostEstimate(flops=0, bytes_accessed=2 * MIB, transcendentals=0),
        name="pack",
    )(block_map, block_owner, line)


def blank_kernel(block_map, out, blank, taken, sem):
    _, child, _ = family()
    blank[...] = jnp.zeros_like(blank)

    @pl.loop(0, 2 * FRONT)
    def _(block):
        taken[block] = 0

    @pl.loop(0, FRONT)
    def _(block):
        taken[block_map[child, block]] = 1

    def copy(block):
        row = pl.multiple_of(block * BLOCK, BLOCK)
        return pltpu.make_async_copy(blank, out.at[pl.ds(row, BLOCK), :], sem)

    @pl.loop(0, 2 * FRONT)
    def _(block):
        @pl.when(taken[block] == 0)
        def _():
            copy(block).start()

    @pl.loop(0, FRONT)
    def _(block):
        copy(0).wait()


PARENT = jax.ShapeDtypeStruct((2 * CONTRIB, SLOTS * BLOCK), jnp.float32)
HELD = pl.BlockSpec(memory_space=pl.ANY)


def blank_rows(block_map):
    return pl.pallas_call(
        blank_kernel,
        out_shape=PARENT,
        in_specs=[SMEM_SPEC],
        out_specs=HELD,
        scratch_shapes=[
            pltpu.VMEM((BLOCK, SLOTS * BLOCK), jnp.float32),
            pltpu.SMEM((2 * FRONT,), jnp.int32),
            pltpu.SemaphoreType.DMA,
        ],
        compiler_params=pltpu.CompilerParams(vmem_limit_bytes=2 * MIB),
        cost_estimate=pl.CostEstimate(flops=0, bytes_accessed=3 * MIB, transcendentals=0),
        name="blank",
    )(block_map)


def place_kernel(chunk, block_map, block_owner, *refs):
    tiles, (out, staged, held, sems) = refs[:SIDE], refs[SIDE + 1 :]
    parent, child, front = family()
    for slot in range(SLOTS):
        held[slot] = 0

    @pl.loop(0, FRONT)
    def _(block):
        slot = block_owner[parent, block_map[child, block]]

        @pl.when(slot // SLOTS == front)
        def _():
            held[lax.rem(slot, SLOTS)] = 1

    none = lax.broadcasted_iota(jnp.int32, (BLOCK, BLOCK), 0) * 0
    copies = []
    for step, tile in enumerate(tiles):
        x = lax.rem(front // SIDE - step + SIDE, SIDE)
        for up, row_z in enumerate(chunk):
            block = x * SIDE + row_z
            here = len(copies)
            for slot in range(SLOTS):
                value = tile[slot, up * BLOCK : (up + 1) * BLOCK, :].astype(jnp.float32)
                staged[here, :, slot * BLOCK : (slot + 1) * BLOCK] = jnp.where(
                    none + held[slot] > 0, value, 0.0
                )
            row = pl.multiple_of(block_map[child, block] * BLOCK, BLOCK)
            copy = pltpu.make_async_copy(
                staged.at[here], out.at[pl.ds(row, BLOCK), :], sems.at[here]
            )
            copy.start()
            copies.append(copy)
    for copy in copies:
        copy.wait()


def place_tiles(chunk, block_map, block_owner, tiles, parent_rows):
    return pl.pallas_call(
        functools.partial(place_kernel, chunk),
        out_shape=PARENT,
        in_specs=[SMEM_SPEC] * 2 + [VMEM_SPEC] * SIDE + [HELD],
        out_specs=HELD,
        scratch_shapes=[
            pltpu.VMEM((len(chunk) * SIDE, BLOCK, SLOTS * BLOCK), jnp.float32),
            pltpu.SMEM((SLOTS,), jnp.int32),
            pltpu.SemaphoreType.DMA((len(chunk) * SIDE,)),
        ],
        input_output_aliases={2 + SIDE: 0},
        compiler_params=pltpu.CompilerParams(vmem_limit_bytes=6 * MIB),
        cost_estimate=pl.CostEstimate(flops=0, bytes_accessed=3 * MIB, transcendentals=0),
        name="place",
    )(block_map, block_owner, *tiles, parent_rows)


def per_device(inv_factors, panel_rows, border, tail, front_sizes, block_map, block_owner):
    inverses = inv_factors[0].reshape(2 * ROWS, PANEL)
    left, right = shift(inverses, "x", 1), shift(inverses, "x", -1)
    up, down, kept = make_messages(tail[0], panel_rows[0])
    low, high = shift(up, "z", 1), shift(down, "z", -1)
    far_first = shift(left[:ROWS], "x", 1)
    far_second = shift(right[ROWS:], "x", -1)
    far_low = shift(low[ON_AT:], "z", 1)
    far_high = shift(high[ON_AT:], "z", -1)

    chunks = spread(lower_chunks(inverses, left, right, far_first, far_second), "z")
    middle = slice(PANEL_AT, ON_AT)
    last = slice(ON_AT, 2 * ROWS)
    panels = [panel_rows[0], low[last], low[middle], high[middle], high[last]]
    panels = spread(jnp.concatenate(panels + [far_low[:HALF], far_high[:HALF]], axis=0), "x")
    blanked = blank_rows(block_map)
    chunks, blanked = lax.optimization_barrier((chunks, blanked))
    link_local, factor_local = eliminate(border[0], chunks, panels)

    rows_z, rows_x = bundle_of(factor_local, "z"), bundle_of(factor_local, "x")
    tails = (kept, low, high, far_low, far_high)

    update = blanked
    for chunk in CHUNKS_OF_ROWS:
        rows = make_tile(chunk, front_sizes, rows_z, rows_x, tails)
        line = bundle_of(to_parent(rows), "z")
        packed = pack_tiles(block_map, block_owner, line)
        tiles = [packed[0]] + [shift(packed[step], "x", step) for step in range(1, SIDE)]
        update = place_tiles(chunk, block_map, block_owner, tiles, update)
    return link_local[None], factor_local[None], update[None]


def solution(mesh):
    return jax.shard_map(
        per_device,
        mesh=mesh,
        in_specs=(
            P("leaf", None, "front", None),
            P("leaf", "front", None),
            P("leaf", "front", None),
            P("leaf", "front", None),
            P(),
            P(),
            P(),
        ),
        out_specs=(P("leaf", "front", None), P("leaf", "front", None), P("leaf", None, "front")),
        check_vma=False,
    )
```

```python
import functools

import jax
import jax.numpy as jnp
from jax import lax
from jax.experimental import pallas as pl
from jax.experimental.pallas import tpu as pltpu
from jax.sharding import PartitionSpec as P

PANEL = 1024
BLOCK = 128
SLOTS = 3
SIDE = 4
FRONT = SIDE * SIDE
CONTRIB = BLOCK * FRONT
ROWS = PANEL // FRONT
MIB = 1024 * 1024


def dot_nt(left, right):
    return lax.dot_general(
        left, right, (((1,), (1,)), ((), ())), preferred_element_type=jnp.float32
    )


def shift(value, axis, by):
    dx, dz = (by, 0) if axis == "x" else (0, by)
    pairs = [
        (x * SIDE + z, (x + dx) % SIDE * SIDE + (z + dz) % SIDE)
        for x in range(SIDE)
        for z in range(SIDE)
    ]
    return lax.ppermute(value, "front", pairs)


def to_parent(value):
    groups = lax.axis_size("leaf")
    return lax.ppermute(
        value, "leaf", [(g, (g + groups // 2) % groups) for g in range(groups)]
    )


RING = (0, -1, 1, 2)


def bundle_of(own, axis):
    half = own.shape[0] // 2
    from_left = shift(own, axis, 1)
    from_right = shift(own, axis, -1)
    far_top = shift(from_left[:half], axis, 1)
    far_bottom = shift(from_right[half:], axis, -1)
    return jnp.concatenate([own, from_left, from_right, far_top, far_bottom], axis=0)


def spread(bundle, axis, *meanwhile):
    half = bundle.shape[0] // 2
    left = shift(bundle, axis, 1)
    right = shift(bundle, axis, -1)
    left, right, meanwhile = lax.optimization_barrier((left, right, meanwhile))
    far_low = shift(left[:half], axis, 1)
    far_high = shift(right[half:], axis, -1)
    return [bundle, left, right, far_low, far_high], *meanwhile


def places(x_first):
    found = []
    for part, second in ((RING, 0), (RING, -1), (RING, 1), (RING[:2], 2), (RING[2:], 2)):
        found.append([(first, second) if x_first else (second, first) for first in part])
    return found


X_FIRST, Z_FIRST = places(True), places(False)


def place_of(front, dx, dz):
    x, z = front // SIDE, front % SIDE
    return lax.rem(x + dx + SIDE, SIDE) * SIDE + lax.rem(z + dz + SIDE, SIDE)


def family():
    groups = lax.axis_size("leaf")
    parent = lax.axis_index("leaf")
    return parent, lax.rem(parent + groups // 2, groups), lax.axis_index("front")


def unpack_inverses(front, bundles, mats):
    z = lax.rem(front, SIDE)
    for bundle, dz, start in zip(bundles, (0, -1, 1, 2, 2), (0, 0, 0, 0, CHUNKS // 2), strict=True):
        place = lax.rem(z + dz + SIDE, SIDE) * ROWS
        for at in range(bundle.shape[0] // (2 * ROWS)):
            x, chunk = LOWER[start + at]
            row = pl.multiple_of(place + x * SIDE * ROWS, ROWS)
            for which in range(2):
                top = (at * 2 + which) * ROWS
                mats[which, pl.ds(row, ROWS), chunk * WIDE : (chunk + 1) * WIDE] = bundle[
                    top : top + ROWS, :
                ]


def unpack_panel(front, sources, mat):
    own, left, right, ahead, behind = sources
    half = 2 * ROWS
    parts = [(own, MIDDLE, 0, 0), (own, ON_AT, 1, 0), (left, ON_AT, 0, -1), (left, MIDDLE, 1, -1)]
    parts += [(right, MIDDLE, 0, 1), (right, ON_AT, 1, 1), (ahead, 0, 0, 2), (behind, 0, 1, 2)]
    for source, top, part, dx in parts:
        for at, dz in enumerate(RING[part * 2 : part * 2 + 2]):
            row = pl.multiple_of(place_of(front, dx, dz) * ROWS, ROWS)
            first = top + at * half // 2
            mat[pl.ds(row, ROWS), :] = source[first : first + ROWS, :]


WIDE = SIDE * ROWS
LOWER = [(x, chunk) for x in range(SIDE) for chunk in range(x + 1)]
CHUNKS = len(LOWER)


def project(rows, inverse, keep):
    for at in range(0, PANEL, WIDE):
        upto = at + WIDE
        keep(at, dot_nt(rows[:, :upto], inverse[at:upto, :upto]))


def lower_kernel(*refs):
    sources, out = refs[:5], refs[5]
    x = lax.axis_index("front") // SIDE
    blocks = [(sources[0], 0, 0), (sources[1], 0, -1), (sources[2], 0, 1)]
    blocks += [(sources[3], 0, 2), (sources[4], 1, 2)]
    for source, first, dx in blocks:
        from_x = lax.rem(x + dx + SIDE, SIDE)
        start = (from_x * (from_x + 1)) // 2
        for chunk in range(SIDE):

            @pl.when(chunk <= from_x)
            def _():
                row = pl.multiple_of((start + chunk) * 2 * ROWS + first * ROWS, ROWS)
                out[pl.ds(row, source.shape[0]), :] = source[:, chunk * WIDE : (chunk + 1) * WIDE]


def lower_chunks(own, left, right, far_first, far_second):
    return pl.pallas_call(
        lower_kernel,
        out_shape=jax.ShapeDtypeStruct((CHUNKS * 2 * ROWS, WIDE), jnp.bfloat16),
        in_specs=[VMEM_SPEC] * 5,
        out_specs=VMEM_SPEC,
        compiler_params=pltpu.CompilerParams(vmem_limit_bytes=4 * MIB),
        cost_estimate=pl.CostEstimate(flops=0, bytes_accessed=MIB, transcendentals=0),
        name="lower",
    )(own, left, right, far_first, far_second)


def panel_kernel(border, *refs):
    inverses, panels, (link_out, factor) = refs[:5], refs[5:10], refs[10:12]
    mats, panel, link, updated = refs[12:]
    front = lax.axis_index("front")
    unpack_inverses(front, inverses, mats)

    def keep_first(at, value):
        factor[:, at : at + WIDE] = value.astype(jnp.bfloat16)

    def keep_link(at, value):
        link[:, at : at + WIDE] = value.astype(jnp.bfloat16)

    def keep_second(at, value):
        factor[:, PANEL + at : PANEL + at + WIDE] = value.astype(jnp.bfloat16)

    project(border, mats.at[0], keep_first)
    unpack_panel(front, panels, panel)
    project(panel, mats.at[0], keep_link)
    link_out[...] = link[pl.ds(pl.multiple_of(front * ROWS, ROWS), ROWS), :]
    for at in range(0, PANEL, WIDE):
        coupled = dot_nt(factor[:, :PANEL], link[at : at + WIDE, :])
        updated[:, at : at + WIDE] = (
            border[:, PANEL + at : PANEL + at + WIDE].astype(jnp.float32) - coupled
        ).astype(jnp.bfloat16)
    project(updated, mats.at[1], keep_second)


VMEM_SPEC = pl.BlockSpec(memory_space=pltpu.VMEM)
SMEM_SPEC = pl.BlockSpec(memory_space=pltpu.SMEM)
HELD = pl.BlockSpec(memory_space=pl.ANY)


def eliminate(border, inverses, panels):
    return pl.pallas_call(
        panel_kernel,
        out_shape=(
            jax.ShapeDtypeStruct((ROWS, PANEL), jnp.bfloat16),
            jax.ShapeDtypeStruct((BLOCK, 2 * PANEL), jnp.bfloat16),
        ),
        in_specs=[VMEM_SPEC] * 11,
        out_specs=(VMEM_SPEC,) * 2,
        scratch_shapes=[
            pltpu.VMEM((2, PANEL, PANEL), jnp.bfloat16),
            pltpu.VMEM((PANEL, PANEL), jnp.bfloat16),
            pltpu.VMEM((PANEL, PANEL), jnp.bfloat16),
            pltpu.VMEM((BLOCK, PANEL), jnp.bfloat16),
        ],
        compiler_params=pltpu.CompilerParams(vmem_limit_bytes=16 * MIB),
        cost_estimate=pl.CostEstimate(
            flops=2 * PANEL**3 + 6 * BLOCK * PANEL**2,
            bytes_accessed=8 * MIB,
            transcendentals=0,
        ),
        name="panels",
    )(border, *inverses, *panels)


LINE = SIDE * BLOCK
CHUNKS_OF_ROWS = ((0, 1), (2, 3))
FIRST, SECOND = CHUNKS_OF_ROWS
GROUPS = (
    [(FIRST, step) for step in range(SIDE)] + [(SECOND, 0)],
    [(SECOND, step) for step in range(1, SIDE)],
)
HALF = ROWS // 2
MIDDLE, ON_AT, LAST, MESSAGE = ROWS, 3 * ROWS, 5 * ROWS, 5 * ROWS + HALF


FOLDED = ((0, 0, ROWS), (1, 0, ROWS), (SIDE - 1, 0, ROWS), (2, 0, HALF), (2, ROWS, HALF))


def fold_kernel(tail, panel_in, inverses_in, folded, panel, inverses):
    x = lax.axis_index("front") // SIDE
    top = 0
    for step, first, height in FOLDED:
        at = pl.multiple_of(lax.rem(x + step, SIDE) * LINE, LINE)
        folded[top : top + height, :LINE] = tail[first : first + height, pl.ds(at, LINE)]
        first += height
        folded[top : top + height, LINE:] = tail[first : first + height, pl.ds(at, LINE)]
        top += height
    panel[...] = panel_in[...]
    inverses[...] = inverses_in[...]


def fold_tail(tail, panel, inverses):
    return pl.pallas_call(
        fold_kernel,
        out_shape=(
            jax.ShapeDtypeStruct((SIDE * ROWS, PANEL), jnp.bfloat16),
            jax.ShapeDtypeStruct(panel.shape, jnp.bfloat16),
            jax.ShapeDtypeStruct(inverses.shape, jnp.bfloat16),
        ),
        in_specs=[VMEM_SPEC] * 3,
        out_specs=(VMEM_SPEC,) * 3,
        compiler_params=pltpu.CompilerParams(vmem_limit_bytes=6 * MIB),
        cost_estimate=pl.CostEstimate(flops=0, bytes_accessed=2 * MIB, transcendentals=0),
        name="fold",
    )(tail, panel, inverses)


def message_kernel(folded, panel, low, high, far_low, far_high, up, down):
    for part, out in enumerate((up, down)):
        first = (part + 1) * ROWS
        out[:ROWS] = folded[first : first + ROWS]
        first = 3 * ROWS + part * HALF
        out[LAST:] = folded[first : first + HALF]
    for out, first, second in ((up, ON_AT, MIDDLE), (down, MIDDLE, ON_AT)):
        out[first : first + ROWS] = panel[...]
        out[first + ROWS : first + 2 * ROWS] = low[...]
        out[second : second + ROWS] = high[...]
        out[second + ROWS : second + ROWS + HALF] = far_low[...]
        out[second + ROWS + HALF : second + 2 * ROWS] = far_high[...]


def make_messages(folded, panels):
    message = jax.ShapeDtypeStruct((MESSAGE, PANEL), jnp.bfloat16)
    return pl.pallas_call(
        message_kernel,
        out_shape=(message, message),
        in_specs=[VMEM_SPEC] * 6,
        out_specs=(VMEM_SPEC,) * 2,
        compiler_params=pltpu.CompilerParams(vmem_limit_bytes=6 * MIB),
        cost_estimate=pl.CostEstimate(flops=0, bytes_accessed=2 * MIB, transcendentals=0),
        name="messages",
    )(folded, *panels)


def tile_kernel(chunk, sizes, rows_x, rows_z, *refs):
    (kept, left, right, ahead, behind), (out, product, tails, rows) = refs[:5], refs[5:]
    front = lax.axis_index("front")
    live = sizes[lax.axis_index("leaf")]
    x, z = front // SIDE, lax.rem(front, SIDE)
    lane = lax.broadcasted_iota(jnp.int32, (BLOCK, BLOCK), 1)
    line = lax.broadcasted_iota(jnp.int32, (BLOCK, BLOCK), 0)
    for step, source in ((0, kept), (1, left), (SIDE - 1, right)):
        tails[step, :ROWS] = source[:ROWS, :LINE]
        tails[step, ROWS:] = source[:ROWS, LINE:]
    for part, source in enumerate((ahead, behind)):
        first = part * ROWS
        tails[2, first : first + HALF] = source[2 * ROWS :, :LINE]
        tails[2, first + HALF : first + ROWS] = source[2 * ROWS :, LINE:]
    for up, row_x in enumerate(chunk):
        away = lax.rem(row_x - x + SIDE, SIDE)
        at = jnp.where(away == 0, 0, jnp.where(away == SIDE - 1, 1, away + 1))
        at = pl.multiple_of(at * BLOCK, BLOCK)
        rows[up * BLOCK : (up + 1) * BLOCK, :] = rows_x[pl.ds(at, BLOCK), :]
    for at in range(0, LINE, WIDE):
        product[:, at : at + WIDE] = dot_nt(rows[...], rows_z[at : at + WIDE, :])
    for up, row_x in enumerate(chunk):
        step = lax.rem(x - row_x + SIDE, SIDE)
        for across, dz in enumerate(RING):
            col_z = lax.rem(z + dz + SIDE, SIDE)
            columns = slice(across * BLOCK, (across + 1) * BLOCK)
            keep = (line + (row_x * SIDE + z) * BLOCK < live) & (
                lane + (x * SIDE + col_z) * BLOCK < live
            )
            old = tails[step, :, pl.ds(pl.multiple_of(col_z * BLOCK, BLOCK), BLOCK)]
            schur = old.astype(jnp.float32) - product[up * BLOCK : (up + 1) * BLOCK, columns]
            out[up * BLOCK : (up + 1) * BLOCK, columns] = jnp.where(keep, schur, 0.0).astype(
                jnp.bfloat16
            )


def make_tile(chunk, sizes, rows_x, rows_z, tails):
    rows = len(chunk) * BLOCK
    return pl.pallas_call(
        functools.partial(tile_kernel, chunk),
        out_shape=jax.ShapeDtypeStruct((rows, LINE), jnp.bfloat16),
        in_specs=[SMEM_SPEC] + [VMEM_SPEC] * 7,
        out_specs=VMEM_SPEC,
        scratch_shapes=[
            pltpu.VMEM((rows, LINE), jnp.float32),
            pltpu.VMEM((SIDE, BLOCK, LINE), jnp.bfloat16),
            pltpu.VMEM((rows, 2 * PANEL), jnp.bfloat16),
        ],
        compiler_params=pltpu.CompilerParams(vmem_limit_bytes=8 * MIB),
        cost_estimate=pl.CostEstimate(
            flops=4 * rows * LINE * PANEL, bytes_accessed=5 * MIB, transcendentals=0
        ),
        name="tile",
    )(sizes, rows_x, rows_z, *tails)


def pack_kernel(plan, line, out):
    rows = line.shape[0] // SIDE
    for at in range(FRONT):

        @pl.when(plan[at] >= 0)
        def _():
            up, across = at // SIDE, at % SIDE
            out[plan[at]] = line[
                up * rows : (up + 1) * rows, across * BLOCK : (across + 1) * BLOCK
            ]


def pack_tiles(plan, line):
    rows = line.shape[0] // SIDE
    return pl.pallas_call(
        pack_kernel,
        out_shape=jax.ShapeDtypeStruct((SIDE * SLOTS, rows, BLOCK), jnp.bfloat16),
        in_specs=[SMEM_SPEC, VMEM_SPEC],
        out_specs=VMEM_SPEC,
        compiler_params=pltpu.CompilerParams(vmem_limit_bytes=4 * MIB),
        cost_estimate=pl.CostEstimate(flops=0, bytes_accessed=6 * MIB, transcendentals=0),
        name="pack",
    )(plan, line)


def blank_kernel(block_map, block_owner, out, plan, blank, taken, sem):
    parent, child, front = family()
    x, z = front // SIDE, lax.rem(front, SIDE)
    blank[...] = jnp.zeros_like(blank)

    @pl.loop(0, 2 * FRONT)
    def _(block):
        taken[block] = 0
        plan[block] = 0

    @pl.loop(0, FRONT)
    def _(block):
        into = block_map[child, block]
        taken[into] = 1
        slot = block_owner[parent, into]

        @pl.when(slot // SLOTS == front)
        def _():
            plan[FRONT + lax.rem(slot, SLOTS)] = 1

    def copy(block):
        row = pl.multiple_of(block * BLOCK, BLOCK)
        return pltpu.make_async_copy(blank, out.at[pl.ds(row, BLOCK), :], sem)

    @pl.loop(0, 2 * FRONT)
    def _(block):
        @pl.when(taken[block] == 0)
        def _():
            copy(block).start()

    for up, dx in enumerate(RING):
        for across, dz in enumerate(RING):
            slot = block_owner[parent, block_map[child, place_of(front, dx, dz)]]
            owner = slot // SLOTS
            step = lax.rem(lax.rem(owner, SIDE) - z + SIDE, SIDE)
            plan[up * SIDE + across] = jnp.where(
                owner // SIDE == x, step * SLOTS + lax.rem(slot, SLOTS), -1
            )

    @pl.loop(0, FRONT)
    def _(block):
        copy(0).wait()


PARENT = jax.ShapeDtypeStruct((2 * CONTRIB, SLOTS * BLOCK), jnp.float32)


def blank_rows(block_map, block_owner):
    return pl.pallas_call(
        blank_kernel,
        out_shape=(PARENT, jax.ShapeDtypeStruct((2 * FRONT,), jnp.int32)),
        in_specs=[SMEM_SPEC] * 2,
        out_specs=(HELD, SMEM_SPEC),
        scratch_shapes=[
            pltpu.VMEM((BLOCK, SLOTS * BLOCK), jnp.float32),
            pltpu.SMEM((2 * FRONT,), jnp.int32),
            pltpu.SemaphoreType.DMA,
        ],
        compiler_params=pltpu.CompilerParams(vmem_limit_bytes=2 * MIB),
        cost_estimate=pl.CostEstimate(flops=0, bytes_accessed=3 * MIB, transcendentals=0),
        name="blank",
    )(block_map, block_owner)


def place_kernel(parts, block_map, plan, *refs):
    tiles, (out, staged, sems) = refs[: len(parts)], refs[len(parts) + 1 :]
    _, child, front = family()
    none = lax.broadcasted_iota(jnp.int32, (BLOCK, BLOCK), 0) * 0
    copies = []
    for (chunk, step), tile in zip(parts, tiles, strict=True):
        z = lax.rem(lax.rem(front, SIDE) - step + SIDE, SIDE)
        for up, row_x in enumerate(chunk):
            here = len(copies)
            for slot in range(SLOTS):
                value = tile[slot, up * BLOCK : (up + 1) * BLOCK, :].astype(jnp.float32)
                staged[here, :, slot * BLOCK : (slot + 1) * BLOCK] = jnp.where(
                    none + plan[FRONT + slot] > 0, value, 0.0
                )
            row = pl.multiple_of(block_map[child, row_x * SIDE + z] * BLOCK, BLOCK)
            copy = pltpu.make_async_copy(
                staged.at[here], out.at[pl.ds(row, BLOCK), :], sems.at[here]
            )
            copy.start()
            copies.append(copy)
    for copy in copies:
        copy.wait()


def place_tiles(block_map, plan, parent_rows, tiles):
    blocks = sum(len(chunk) for chunk, _ in tiles)
    return pl.pallas_call(
        functools.partial(place_kernel, list(tiles)),
        out_shape=PARENT,
        in_specs=[SMEM_SPEC] * 2 + [VMEM_SPEC] * len(tiles) + [HELD],
        out_specs=HELD,
        scratch_shapes=[
            pltpu.VMEM((blocks, BLOCK, SLOTS * BLOCK), jnp.float32),
            pltpu.SemaphoreType.DMA((blocks,)),
        ],
        input_output_aliases={2 + len(tiles): 0},
        compiler_params=pltpu.CompilerParams(vmem_limit_bytes=6 * MIB),
        cost_estimate=pl.CostEstimate(flops=0, bytes_accessed=MIB, transcendentals=0),
        name="place",
    )(block_map, plan, *tiles.values(), parent_rows)


def per_device(inv_factors, panel_rows, border, tail, front_sizes, block_map, block_owner):
    inverses, panel = inv_factors[0].reshape(2 * ROWS, PANEL), panel_rows[0]
    left, right = shift(inverses, "x", 1), shift(inverses, "x", -1)
    low, high = shift(panel, "z", 1), shift(panel, "z", -1)
    folded, panel, inverses = fold_tail(tail[0], panel, inverses)
    low, high, folded, panel, inverses = lax.optimization_barrier(
        (low, high, folded, panel, inverses)
    )
    far_first = shift(left[:ROWS], "x", 1)
    far_second = shift(right[ROWS:], "x", -1)
    far_low = shift(low[:HALF], "z", 1)
    far_high = shift(high[HALF:], "z", -1)

    chunks = lower_chunks(inverses, left, right, far_first, far_second)
    chunks, update, plan = spread(chunks, "z", *blank_rows(block_map, block_owner))
    up, down = make_messages(folded, (panel, low, high, far_low, far_high))
    from_left, from_right = shift(up, "x", 1), shift(down, "x", -1)
    ahead = shift(from_left[ON_AT:], "x", 1)
    behind = shift(from_right[ON_AT:], "x", -1)
    panels = (down, from_left, from_right, ahead, behind)
    link_local, factor_local = eliminate(border[0], chunks, panels)

    rows_x, rows_z = bundle_of(factor_local, "x"), bundle_of(factor_local, "z")
    tails = (folded, from_left, from_right, ahead, behind)

    tiles = {}
    for chunk in CHUNKS_OF_ROWS:
        rows = make_tile(chunk, front_sizes, rows_x, rows_z, tails)
        packed = pack_tiles(plan, bundle_of(to_parent(rows), "x"))
        for step in range(SIDE):
            tile = packed[step * SLOTS : (step + 1) * SLOTS]
            tiles[chunk, step] = shift(tile, "z", step) if step else tile
    for group in GROUPS:
        update = place_tiles(block_map, plan, update, {key: tiles[key] for key in group})
    return link_local[None], factor_local[None], update[None]


def solution(mesh):
    return jax.shard_map(
        per_device,
        mesh=mesh,
        in_specs=(
            P("leaf", None, "front", None),
            P("leaf", "front", None),
            P("leaf", "front", None),
            P("leaf", "front", None),
            P(),
            P(),
            P(),
        ),
        out_specs=(P("leaf", "front", None), P("leaf", "front", None), P("leaf", None, "front")),
        check_vma=False,
    )
```

```python
import functools

import jax
import jax.numpy as jnp
from jax import lax
from jax.experimental import pallas as pl
from jax.experimental.pallas import tpu as pltpu
from jax.sharding import PartitionSpec as P

PANEL = 1024
BLOCK = 128
SLOTS = 3
SIDE = 4
FRONT = SIDE * SIDE
CONTRIB = BLOCK * FRONT
ROWS = PANEL // FRONT
MIB = 1024 * 1024


def dot_nt(left, right):
    return lax.dot_general(
        left, right, (((1,), (1,)), ((), ())), preferred_element_type=jnp.float32
    )


def shift(value, axis, by):
    dx, dz = (by, 0) if axis == "x" else (0, by)
    pairs = [
        (x * SIDE + z, (x + dx) % SIDE * SIDE + (z + dz) % SIDE)
        for x in range(SIDE)
        for z in range(SIDE)
    ]
    return lax.ppermute(value, "front", pairs)


def to_parent(value):
    groups = lax.axis_size("leaf")
    return lax.ppermute(
        value, "leaf", [(g, (g + groups // 2) % groups) for g in range(groups)]
    )


RING = (0, -1, 1, 2)


def bundle_of(own, axis):
    half = own.shape[0] // 2
    from_left = shift(own, axis, 1)
    from_right = shift(own, axis, -1)
    far_top = shift(from_left[:half], axis, 1)
    far_bottom = shift(from_right[half:], axis, -1)
    return jnp.concatenate([own, from_left, from_right, far_top, far_bottom], axis=0)


def spread(bundle, axis, *meanwhile):
    half = bundle.shape[0] // 2
    left = shift(bundle, axis, 1)
    right = shift(bundle, axis, -1)
    left, right, meanwhile = lax.optimization_barrier((left, right, meanwhile))
    far_low = shift(left[:half], axis, 1)
    far_high = shift(right[half:], axis, -1)
    return [bundle, left, right, far_low, far_high], *meanwhile


def places(x_first):
    found = []
    for part, second in ((RING, 0), (RING, -1), (RING, 1), (RING[:2], 2), (RING[2:], 2)):
        found.append([(first, second) if x_first else (second, first) for first in part])
    return found


X_FIRST, Z_FIRST = places(True), places(False)


def place_of(front, dx, dz):
    x, z = front // SIDE, front % SIDE
    return lax.rem(x + dx + SIDE, SIDE) * SIDE + lax.rem(z + dz + SIDE, SIDE)


def family():
    groups = lax.axis_size("leaf")
    parent = lax.axis_index("leaf")
    return parent, lax.rem(parent + groups // 2, groups), lax.axis_index("front")


def unpack_inverses(front, bundles, mats):
    z = lax.rem(front, SIDE)
    for bundle, dz, start in zip(bundles, (0, -1, 1, 2, 2), (0, 0, 0, 0, CHUNKS // 2), strict=True):
        place = lax.rem(z + dz + SIDE, SIDE) * ROWS
        for at in range(bundle.shape[0] // (2 * ROWS)):
            x, chunk = LOWER[start + at]
            row = pl.multiple_of(place + x * SIDE * ROWS, ROWS)
            for which in range(2):
                top = (at * 2 + which) * ROWS
                mats[which, pl.ds(row, ROWS), chunk * WIDE : (chunk + 1) * WIDE] = bundle[
                    top : top + ROWS, :
                ]


def unpack_panel(front, sources, mat):
    own, left, right, ahead, behind = sources
    half = 2 * ROWS
    parts = [(own, MIDDLE, 0, 0), (own, ON_AT, 1, 0), (left, ON_AT, 0, -1), (left, MIDDLE, 1, -1)]
    parts += [(right, MIDDLE, 0, 1), (right, ON_AT, 1, 1), (ahead, 0, 0, 2), (behind, 0, 1, 2)]
    for source, top, part, dx in parts:
        for at, dz in enumerate(RING[part * 2 : part * 2 + 2]):
            row = pl.multiple_of(place_of(front, dx, dz) * ROWS, ROWS)
            first = top + at * half // 2
            mat[pl.ds(row, ROWS), :] = source[first : first + ROWS, :]


WIDE = SIDE * ROWS
TALL = 576
LOWER = [(x, chunk) for x in range(SIDE) for chunk in range(x + 1)]
CHUNKS = len(LOWER)


def project(rows, inverse, keep):
    for at in range(0, PANEL, WIDE):
        upto = at + WIDE
        keep(at, dot_nt(rows[:, :upto], inverse[at:upto, :upto]))


def lower_kernel(*refs):
    sources, out = refs[:5], refs[5]
    x = lax.axis_index("front") // SIDE
    blocks = [(sources[0], 0, 0), (sources[1], 0, -1), (sources[2], 0, 1)]
    blocks += [(sources[3], 0, 2), (sources[4], 1, 2)]
    for source, first, dx in blocks:
        from_x = lax.rem(x + dx + SIDE, SIDE)
        start = (from_x * (from_x + 1)) // 2
        for chunk in range(SIDE):

            @pl.when(chunk <= from_x)
            def _():
                row = pl.multiple_of((start + chunk) * 2 * ROWS + first * ROWS, ROWS)
                out[pl.ds(row, source.shape[0]), :] = source[:, chunk * WIDE : (chunk + 1) * WIDE]


def lower_chunks(own, left, right, far_first, far_second):
    return pl.pallas_call(
        lower_kernel,
        out_shape=jax.ShapeDtypeStruct((CHUNKS * 2 * ROWS, WIDE), jnp.bfloat16),
        in_specs=[VMEM_SPEC] * 5,
        out_specs=VMEM_SPEC,
        compiler_params=pltpu.CompilerParams(vmem_limit_bytes=4 * MIB),
        cost_estimate=pl.CostEstimate(flops=0, bytes_accessed=MIB, transcendentals=0),
        name="lower",
    )(own, left, right, far_first, far_second)


def panel_kernel(border, *refs):
    inverses, panels, (link_out, factor) = refs[:5], refs[5:10], refs[10:12]
    mats, both, link, updated = refs[12:]
    front = lax.axis_index("front")
    unpack_inverses(front, inverses, mats)

    both[:BLOCK] = border[:, :PANEL]
    unpack_panel(front, panels, both.at[BLOCK:])

    def keep_both(up):
        def keep(at, value):
            if up == 0:
                factor[:, at : at + WIDE] = value[:BLOCK].astype(jnp.bfloat16)
                value = value[BLOCK:]
            first = max(up - BLOCK, 0)
            link[first : first + value.shape[0], at : at + WIDE] = value.astype(jnp.bfloat16)

        return keep

    def keep_second(at, value):
        factor[:, PANEL + at : PANEL + at + WIDE] = value.astype(jnp.bfloat16)

    for up in range(0, BLOCK + PANEL, TALL):
        project(both.at[up : up + TALL], mats.at[0], keep_both(up))
    link_out[...] = link[pl.ds(pl.multiple_of(front * ROWS, ROWS), ROWS), :]
    for at in range(0, PANEL, WIDE):
        coupled = dot_nt(factor[:, :PANEL], link[at : at + WIDE, :])
        updated[:, at : at + WIDE] = (
            border[:, PANEL + at : PANEL + at + WIDE].astype(jnp.float32) - coupled
        ).astype(jnp.bfloat16)
    project(updated, mats.at[1], keep_second)


VMEM_SPEC = pl.BlockSpec(memory_space=pltpu.VMEM)
SMEM_SPEC = pl.BlockSpec(memory_space=pltpu.SMEM)
HELD = pl.BlockSpec(memory_space=pl.ANY)


def eliminate(border, inverses, panels):
    return pl.pallas_call(
        panel_kernel,
        out_shape=(
            jax.ShapeDtypeStruct((ROWS, PANEL), jnp.bfloat16),
            jax.ShapeDtypeStruct((BLOCK, 2 * PANEL), jnp.bfloat16),
        ),
        in_specs=[VMEM_SPEC] * 11,
        out_specs=(VMEM_SPEC,) * 2,
        scratch_shapes=[
            pltpu.VMEM((2, PANEL, PANEL), jnp.bfloat16),
            pltpu.VMEM((BLOCK + PANEL, PANEL), jnp.bfloat16),
            pltpu.VMEM((PANEL, PANEL), jnp.bfloat16),
            pltpu.VMEM((BLOCK, PANEL), jnp.bfloat16),
        ],
        compiler_params=pltpu.CompilerParams(vmem_limit_bytes=16 * MIB),
        cost_estimate=pl.CostEstimate(
            flops=2 * PANEL**3 + 6 * BLOCK * PANEL**2,
            bytes_accessed=8 * MIB,
            transcendentals=0,
        ),
        name="panels",
    )(border, *inverses, *panels)


LINE = SIDE * BLOCK
CHUNKS_OF_ROWS = ((0, 1), (2, 3))
FIRST, SECOND = CHUNKS_OF_ROWS
GROUPS = (
    [(FIRST, step) for step in range(SIDE)] + [(SECOND, 0)],
    [(SECOND, step) for step in range(1, SIDE)],
)
HALF = ROWS // 2
MIDDLE, ON_AT, LAST, MESSAGE = ROWS, 3 * ROWS, 5 * ROWS, 5 * ROWS + HALF


FOLDED = ((0, 0, ROWS), (1, 0, ROWS), (SIDE - 1, 0, ROWS), (2, 0, HALF), (2, ROWS, HALF))


def fold_kernel(tail, panel_in, inverses_in, folded, panel, inverses):
    x = lax.axis_index("front") // SIDE
    top = 0
    for step, first, height in FOLDED:
        at = pl.multiple_of(lax.rem(x + step, SIDE) * LINE, LINE)
        folded[top : top + height, :LINE] = tail[first : first + height, pl.ds(at, LINE)]
        first += height
        folded[top : top + height, LINE:] = tail[first : first + height, pl.ds(at, LINE)]
        top += height
    panel[...] = panel_in[...]
    inverses[...] = inverses_in[...]


def fold_tail(tail, panel, inverses):
    return pl.pallas_call(
        fold_kernel,
        out_shape=(
            jax.ShapeDtypeStruct((SIDE * ROWS, PANEL), jnp.bfloat16),
            jax.ShapeDtypeStruct(panel.shape, jnp.bfloat16),
            jax.ShapeDtypeStruct(inverses.shape, jnp.bfloat16),
        ),
        in_specs=[VMEM_SPEC] * 3,
        out_specs=(VMEM_SPEC,) * 3,
        compiler_params=pltpu.CompilerParams(vmem_limit_bytes=6 * MIB),
        cost_estimate=pl.CostEstimate(flops=0, bytes_accessed=2 * MIB, transcendentals=0),
        name="fold",
    )(tail, panel, inverses)


def message_kernel(folded, panel, low, high, far_low, far_high, up, down):
    for part, out in enumerate((up, down)):
        first = (part + 1) * ROWS
        out[:ROWS] = folded[first : first + ROWS]
        first = 3 * ROWS + part * HALF
        out[LAST:] = folded[first : first + HALF]
    for out, first, second in ((up, ON_AT, MIDDLE), (down, MIDDLE, ON_AT)):
        out[first : first + ROWS] = panel[...]
        out[first + ROWS : first + 2 * ROWS] = low[...]
        out[second : second + ROWS] = high[...]
        out[second + ROWS : second + ROWS + HALF] = far_low[...]
        out[second + ROWS + HALF : second + 2 * ROWS] = far_high[...]


def make_messages(folded, panels):
    message = jax.ShapeDtypeStruct((MESSAGE, PANEL), jnp.bfloat16)
    return pl.pallas_call(
        message_kernel,
        out_shape=(message, message),
        in_specs=[VMEM_SPEC] * 6,
        out_specs=(VMEM_SPEC,) * 2,
        compiler_params=pltpu.CompilerParams(vmem_limit_bytes=6 * MIB),
        cost_estimate=pl.CostEstimate(flops=0, bytes_accessed=2 * MIB, transcendentals=0),
        name="messages",
    )(folded, *panels)


def tile_kernel(chunk, sizes, rows_x, rows_z, *refs):
    (kept, left, right, ahead, behind), (out, product, tails, rows) = refs[:5], refs[5:]
    front = lax.axis_index("front")
    live = sizes[lax.axis_index("leaf")]
    x, z = front // SIDE, lax.rem(front, SIDE)
    lane = lax.broadcasted_iota(jnp.int32, (BLOCK, BLOCK), 1)
    line = lax.broadcasted_iota(jnp.int32, (BLOCK, BLOCK), 0)
    for step, source in ((0, kept), (1, left), (SIDE - 1, right)):
        tails[step, :ROWS] = source[:ROWS, :LINE]
        tails[step, ROWS:] = source[:ROWS, LINE:]
    for part, source in enumerate((ahead, behind)):
        first = part * ROWS
        tails[2, first : first + HALF] = source[2 * ROWS :, :LINE]
        tails[2, first + HALF : first + ROWS] = source[2 * ROWS :, LINE:]
    for up, row_x in enumerate(chunk):
        away = lax.rem(row_x - x + SIDE, SIDE)
        at = jnp.where(away == 0, 0, jnp.where(away == SIDE - 1, 1, away + 1))
        at = pl.multiple_of(at * BLOCK, BLOCK)
        rows[up * BLOCK : (up + 1) * BLOCK, :] = rows_x[pl.ds(at, BLOCK), :]
    for at in range(0, LINE, WIDE):
        product[:, at : at + WIDE] = dot_nt(rows[...], rows_z[at : at + WIDE, :])
    for up, row_x in enumerate(chunk):
        step = lax.rem(x - row_x + SIDE, SIDE)
        for across, dz in enumerate(RING):
            col_z = lax.rem(z + dz + SIDE, SIDE)
            columns = slice(across * BLOCK, (across + 1) * BLOCK)
            keep = (line + (row_x * SIDE + z) * BLOCK < live) & (
                lane + (x * SIDE + col_z) * BLOCK < live
            )
            old = tails[step, :, pl.ds(pl.multiple_of(col_z * BLOCK, BLOCK), BLOCK)]
            schur = old.astype(jnp.float32) - product[up * BLOCK : (up + 1) * BLOCK, columns]
            out[up * BLOCK : (up + 1) * BLOCK, columns] = jnp.where(keep, schur, 0.0).astype(
                jnp.bfloat16
            )


def make_tile(chunk, sizes, rows_x, rows_z, tails):
    rows = len(chunk) * BLOCK
    return pl.pallas_call(
        functools.partial(tile_kernel, chunk),
        out_shape=jax.ShapeDtypeStruct((rows, LINE), jnp.bfloat16),
        in_specs=[SMEM_SPEC] + [VMEM_SPEC] * 7,
        out_specs=VMEM_SPEC,
        scratch_shapes=[
            pltpu.VMEM((rows, LINE), jnp.float32),
            pltpu.VMEM((SIDE, BLOCK, LINE), jnp.bfloat16),
            pltpu.VMEM((rows, 2 * PANEL), jnp.bfloat16),
        ],
        compiler_params=pltpu.CompilerParams(vmem_limit_bytes=8 * MIB),
        cost_estimate=pl.CostEstimate(
            flops=4 * rows * LINE * PANEL, bytes_accessed=5 * MIB, transcendentals=0
        ),
        name="tile",
    )(sizes, rows_x, rows_z, *tails)


def pack_kernel(plan, line, out):
    rows = line.shape[0] // SIDE
    for at in range(FRONT):

        @pl.when(plan[at] >= 0)
        def _():
            up, across = at // SIDE, at % SIDE
            out[plan[at]] = line[
                up * rows : (up + 1) * rows, across * BLOCK : (across + 1) * BLOCK
            ]


def pack_tiles(plan, line):
    rows = line.shape[0] // SIDE
    return pl.pallas_call(
        pack_kernel,
        out_shape=jax.ShapeDtypeStruct((SIDE * SLOTS, rows, BLOCK), jnp.bfloat16),
        in_specs=[SMEM_SPEC, VMEM_SPEC],
        out_specs=VMEM_SPEC,
        compiler_params=pltpu.CompilerParams(vmem_limit_bytes=4 * MIB),
        cost_estimate=pl.CostEstimate(flops=0, bytes_accessed=6 * MIB, transcendentals=0),
        name="pack",
    )(plan, line)


def blank_kernel(block_map, block_owner, out, plan, blank, taken, sem):
    parent, child, front = family()
    x, z = front // SIDE, lax.rem(front, SIDE)
    blank[...] = jnp.zeros_like(blank)

    @pl.loop(0, 2 * FRONT)
    def _(block):
        taken[block] = 0
        plan[block] = 0

    @pl.loop(0, FRONT)
    def _(block):
        into = block_map[child, block]
        taken[into] = 1
        slot = block_owner[parent, into]

        @pl.when(slot // SLOTS == front)
        def _():
            plan[FRONT + lax.rem(slot, SLOTS)] = 1

    def copy(block):
        row = pl.multiple_of(block * BLOCK, BLOCK)
        return pltpu.make_async_copy(blank, out.at[pl.ds(row, BLOCK), :], sem)

    @pl.loop(0, 2 * FRONT)
    def _(block):
        @pl.when(taken[block] == 0)
        def _():
            copy(block).start()

    for up, dx in enumerate(RING):
        for across, dz in enumerate(RING):
            slot = block_owner[parent, block_map[child, place_of(front, dx, dz)]]
            owner = slot // SLOTS
            step = lax.rem(lax.rem(owner, SIDE) - z + SIDE, SIDE)
            plan[up * SIDE + across] = jnp.where(
                owner // SIDE == x, step * SLOTS + lax.rem(slot, SLOTS), -1
            )

    @pl.loop(0, FRONT)
    def _(block):
        copy(0).wait()


PARENT = jax.ShapeDtypeStruct((2 * CONTRIB, SLOTS * BLOCK), jnp.float32)


def blank_rows(block_map, block_owner):
    return pl.pallas_call(
        blank_kernel,
        out_shape=(PARENT, jax.ShapeDtypeStruct((2 * FRONT,), jnp.int32)),
        in_specs=[SMEM_SPEC] * 2,
        out_specs=(HELD, SMEM_SPEC),
        scratch_shapes=[
            pltpu.VMEM((BLOCK, SLOTS * BLOCK), jnp.float32),
            pltpu.SMEM((2 * FRONT,), jnp.int32),
            pltpu.SemaphoreType.DMA,
        ],
        compiler_params=pltpu.CompilerParams(vmem_limit_bytes=2 * MIB),
        cost_estimate=pl.CostEstimate(flops=0, bytes_accessed=3 * MIB, transcendentals=0),
        name="blank",
    )(block_map, block_owner)


def place_kernel(parts, block_map, plan, *refs):
    tiles, (out, staged, sems) = refs[: len(parts)], refs[len(parts) + 1 :]
    _, child, front = family()
    none = lax.broadcasted_iota(jnp.int32, (BLOCK, BLOCK), 0) * 0
    copies = []
    for (chunk, step), tile in zip(parts, tiles, strict=True):
        z = lax.rem(lax.rem(front, SIDE) - step + SIDE, SIDE)
        for up, row_x in enumerate(chunk):
            here = len(copies)
            for slot in range(SLOTS):
                value = tile[slot, up * BLOCK : (up + 1) * BLOCK, :].astype(jnp.float32)
                staged[here, :, slot * BLOCK : (slot + 1) * BLOCK] = jnp.where(
                    none + plan[FRONT + slot] > 0, value, 0.0
                )
            row = pl.multiple_of(block_map[child, row_x * SIDE + z] * BLOCK, BLOCK)
            copy = pltpu.make_async_copy(
                staged.at[here], out.at[pl.ds(row, BLOCK), :], sems.at[here]
            )
            copy.start()
            copies.append(copy)
    for copy in copies:
        copy.wait()


def place_tiles(block_map, plan, parent_rows, tiles):
    blocks = sum(len(chunk) for chunk, _ in tiles)
    return pl.pallas_call(
        functools.partial(place_kernel, list(tiles)),
        out_shape=PARENT,
        in_specs=[SMEM_SPEC] * 2 + [VMEM_SPEC] * len(tiles) + [HELD],
        out_specs=HELD,
        scratch_shapes=[
            pltpu.VMEM((blocks, BLOCK, SLOTS * BLOCK), jnp.float32),
            pltpu.SemaphoreType.DMA((blocks,)),
        ],
        input_output_aliases={2 + len(tiles): 0},
        compiler_params=pltpu.CompilerParams(vmem_limit_bytes=6 * MIB),
        cost_estimate=pl.CostEstimate(flops=0, bytes_accessed=MIB, transcendentals=0),
        name="place",
    )(block_map, plan, *tiles.values(), parent_rows)


def per_device(inv_factors, panel_rows, border, tail, front_sizes, block_map, block_owner):
    inverses, panel = inv_factors[0].reshape(2 * ROWS, PANEL), panel_rows[0]
    left, right = shift(inverses, "x", 1), shift(inverses, "x", -1)
    low, high = shift(panel, "z", 1), shift(panel, "z", -1)
    folded, panel, inverses = fold_tail(tail[0], panel, inverses)
    low, high, folded, panel, inverses = lax.optimization_barrier(
        (low, high, folded, panel, inverses)
    )
    far_first = shift(left[:ROWS], "x", 1)
    far_second = shift(right[ROWS:], "x", -1)
    far_low = shift(low[:HALF], "z", 1)
    far_high = shift(high[HALF:], "z", -1)

    chunks = lower_chunks(inverses, left, right, far_first, far_second)
    chunks, update, plan = spread(chunks, "z", *blank_rows(block_map, block_owner))
    up, down = make_messages(folded, (panel, low, high, far_low, far_high))
    from_left, from_right = shift(up, "x", 1), shift(down, "x", -1)
    ahead = shift(from_left[ON_AT:], "x", 1)
    behind = shift(from_right[ON_AT:], "x", -1)
    panels = (down, from_left, from_right, ahead, behind)
    link_local, factor_local = eliminate(border[0], chunks, panels)

    rows_x, rows_z = bundle_of(factor_local, "x"), bundle_of(factor_local, "z")
    rows_x, rows_z = lax.optimization_barrier((rows_x, rows_z))
    factor_local = rows_z[:BLOCK]
    tails = (folded, from_left, from_right, ahead, behind)

    tiles = {}
    for chunk in CHUNKS_OF_ROWS:
        rows = make_tile(chunk, front_sizes, rows_x, rows_z, tails)
        there = to_parent(rows)
        if chunk is FIRST:
            there, factor_local = lax.optimization_barrier((there, factor_local))
        packed = pack_tiles(plan, bundle_of(there, "x"))
        for step in range(SIDE):
            tile = packed[step * SLOTS : (step + 1) * SLOTS]
            tiles[chunk, step] = shift(tile, "z", step) if step else tile
    for group in GROUPS:
        update = place_tiles(block_map, plan, update, {key: tiles[key] for key in group})
    return link_local[None], factor_local[None], update[None]


def solution(mesh):
    return jax.shard_map(
        per_device,
        mesh=mesh,
        in_specs=(
            P("leaf", None, "front", None),
            P("leaf", "front", None),
            P("leaf", "front", None),
            P("leaf", "front", None),
            P(),
            P(),
            P(),
        ),
        out_specs=(P("leaf", "front", None), P("leaf", "front", None), P("leaf", None, "front")),
        check_vma=False,
    )
```

```python
import functools

import jax
import jax.numpy as jnp
from jax import lax
from jax.experimental import pallas as pl
from jax.experimental.pallas import tpu as pltpu
from jax.sharding import PartitionSpec as P

PANEL = 1024
BLOCK = 128
SLOTS = 3
SIDE = 4
FRONT = SIDE * SIDE
CONTRIB = BLOCK * FRONT
ROWS = PANEL // FRONT
MIB = 1024 * 1024


def dot_nt(left, right):
    return lax.dot_general(
        left, right, (((1,), (1,)), ((), ())), preferred_element_type=jnp.float32
    )


def shift(value, axis, by):
    dx, dz = (by, 0) if axis == "x" else (0, by)
    pairs = [
        (x * SIDE + z, (x + dx) % SIDE * SIDE + (z + dz) % SIDE)
        for x in range(SIDE)
        for z in range(SIDE)
    ]
    return lax.ppermute(value, "front", pairs)


def to_parent(value):
    groups = lax.axis_size("leaf")
    return lax.ppermute(
        value, "leaf", [(g, (g + groups // 2) % groups) for g in range(groups)]
    )


RING = (0, -1, 1, 2)


def bundle_of(own, axis):
    half = own.shape[0] // 2
    from_left = shift(own, axis, 1)
    from_right = shift(own, axis, -1)
    far_top = shift(from_left[:half], axis, 1)
    far_bottom = shift(from_right[half:], axis, -1)
    return jnp.concatenate([own, from_left, from_right, far_top, far_bottom], axis=0)


def spread(bundle, axis, *meanwhile):
    half = bundle.shape[0] // 2
    left = shift(bundle, axis, 1)
    right = shift(bundle, axis, -1)
    left, right, meanwhile = lax.optimization_barrier((left, right, meanwhile))
    far_low = shift(left[:half], axis, 1)
    far_high = shift(right[half:], axis, -1)
    return [bundle, left, right, far_low, far_high], *meanwhile


def places(x_first):
    found = []
    for part, second in ((RING, 0), (RING, -1), (RING, 1), (RING[:2], 2), (RING[2:], 2)):
        found.append([(first, second) if x_first else (second, first) for first in part])
    return found


X_FIRST, Z_FIRST = places(True), places(False)


def place_of(front, dx, dz):
    x, z = front // SIDE, front % SIDE
    return lax.rem(x + dx + SIDE, SIDE) * SIDE + lax.rem(z + dz + SIDE, SIDE)


def family():
    groups = lax.axis_size("leaf")
    parent = lax.axis_index("leaf")
    return parent, lax.rem(parent + groups // 2, groups), lax.axis_index("front")


def unpack_inverses(front, bundles, mats):
    z = lax.rem(front, SIDE)
    for bundle, dz, start in zip(bundles, (0, -1, 1, 2, 2), (0, 0, 0, 0, CHUNKS // 2), strict=True):
        place = lax.rem(z + dz + SIDE, SIDE) * ROWS
        for at in range(bundle.shape[0] // (2 * ROWS)):
            x, chunk = LOWER[start + at]
            row = pl.multiple_of(place + x * SIDE * ROWS, ROWS)
            for which in range(2):
                top = (at * 2 + which) * ROWS
                mats[which, pl.ds(row, ROWS), chunk * WIDE : (chunk + 1) * WIDE] = bundle[
                    top : top + ROWS, :
                ]


def unpack_panel(front, sources, mat):
    own, left, right, ahead, behind = sources
    half = 2 * ROWS
    parts = [(own, MIDDLE, 0, 0), (own, ON_AT, 1, 0), (left, ON_AT, 0, -1), (left, MIDDLE, 1, -1)]
    parts += [(right, MIDDLE, 0, 1), (right, ON_AT, 1, 1), (ahead, 0, 0, 2), (behind, 0, 1, 2)]
    for source, top, part, dx in parts:
        for at, dz in enumerate(RING[part * 2 : part * 2 + 2]):
            row = pl.multiple_of(place_of(front, dx, dz) * ROWS, ROWS)
            first = top + at * half // 2
            mat[pl.ds(row, ROWS), :] = source[first : first + ROWS, :]


WIDE = SIDE * ROWS
TALL = 576
LOWER = [(x, chunk) for x in range(SIDE) for chunk in range(x + 1)]
CHUNKS = len(LOWER)


def project(rows, inverse, keep):
    for at in range(0, PANEL, WIDE):
        upto = at + WIDE
        keep(at, dot_nt(rows[:, :upto], inverse[at:upto, :upto]))


def lower_kernel(*refs):
    sources, out = refs[:5], refs[5]
    x = lax.axis_index("front") // SIDE
    blocks = [(sources[0], 0, 0), (sources[1], 0, -1), (sources[2], 0, 1)]
    blocks += [(sources[3], 0, 2), (sources[4], 1, 2)]
    for source, first, dx in blocks:
        from_x = lax.rem(x + dx + SIDE, SIDE)
        start = (from_x * (from_x + 1)) // 2
        for chunk in range(SIDE):

            @pl.when(chunk <= from_x)
            def _():
                row = pl.multiple_of((start + chunk) * 2 * ROWS + first * ROWS, ROWS)
                out[pl.ds(row, source.shape[0]), :] = source[:, chunk * WIDE : (chunk + 1) * WIDE]


def lower_chunks(own, left, right, far_first, far_second):
    return pl.pallas_call(
        lower_kernel,
        out_shape=jax.ShapeDtypeStruct((CHUNKS * 2 * ROWS, WIDE), jnp.bfloat16),
        in_specs=[VMEM_SPEC] * 5,
        out_specs=VMEM_SPEC,
        compiler_params=pltpu.CompilerParams(vmem_limit_bytes=4 * MIB),
        cost_estimate=pl.CostEstimate(flops=0, bytes_accessed=MIB, transcendentals=0),
        name="lower",
    )(own, left, right, far_first, far_second)


def panel_kernel(border, *refs):
    inverses, panels, (link_out, factor) = refs[:5], refs[5:10], refs[10:12]
    mats, both, link, updated = refs[12:]
    front = lax.axis_index("front")
    unpack_inverses(front, inverses, mats)

    both[:BLOCK] = border[:, :PANEL]
    unpack_panel(front, panels, both.at[BLOCK:])

    def keep_both(up):
        def keep(at, value):
            if up == 0:
                factor[:, at : at + WIDE] = value[:BLOCK].astype(jnp.bfloat16)
                value = value[BLOCK:]
            first = max(up - BLOCK, 0)
            link[first : first + value.shape[0], at : at + WIDE] = value.astype(jnp.bfloat16)

        return keep

    def keep_second(at, value):
        factor[:, PANEL + at : PANEL + at + WIDE] = value.astype(jnp.bfloat16)

    for up in range(0, BLOCK + PANEL, TALL):
        project(both.at[up : up + TALL], mats.at[0], keep_both(up))
    link_out[...] = link[pl.ds(pl.multiple_of(front * ROWS, ROWS), ROWS), :]
    for at in range(0, PANEL, WIDE):
        coupled = dot_nt(factor[:, :PANEL], link[at : at + WIDE, :])
        updated[:, at : at + WIDE] = (
            border[:, PANEL + at : PANEL + at + WIDE].astype(jnp.float32) - coupled
        ).astype(jnp.bfloat16)
    project(updated, mats.at[1], keep_second)


VMEM_SPEC = pl.BlockSpec(memory_space=pltpu.VMEM)
SMEM_SPEC = pl.BlockSpec(memory_space=pltpu.SMEM)
HELD = pl.BlockSpec(memory_space=pl.ANY)


def eliminate(border, inverses, panels):
    return pl.pallas_call(
        panel_kernel,
        out_shape=(
            jax.ShapeDtypeStruct((ROWS, PANEL), jnp.bfloat16),
            jax.ShapeDtypeStruct((BLOCK, 2 * PANEL), jnp.bfloat16),
        ),
        in_specs=[VMEM_SPEC] * 11,
        out_specs=(VMEM_SPEC,) * 2,
        scratch_shapes=[
            pltpu.VMEM((2, PANEL, PANEL), jnp.bfloat16),
            pltpu.VMEM((BLOCK + PANEL, PANEL), jnp.bfloat16),
            pltpu.VMEM((PANEL, PANEL), jnp.bfloat16),
            pltpu.VMEM((BLOCK, PANEL), jnp.bfloat16),
        ],
        compiler_params=pltpu.CompilerParams(vmem_limit_bytes=16 * MIB),
        cost_estimate=pl.CostEstimate(
            flops=2 * PANEL**3 + 6 * BLOCK * PANEL**2,
            bytes_accessed=8 * MIB,
            transcendentals=0,
        ),
        name="panels",
    )(border, *inverses, *panels)


LINE = SIDE * BLOCK
CHUNKS_OF_ROWS = ((0, 1), (2, 3))
FIRST, SECOND = CHUNKS_OF_ROWS
GROUPS = (
    [(FIRST, step) for step in range(SIDE)] + [(SECOND, 0)],
    [(SECOND, step) for step in range(1, SIDE)],
)
HALF = ROWS // 2
MIDDLE, ON_AT, LAST, MESSAGE = ROWS, 3 * ROWS, 5 * ROWS, 5 * ROWS + HALF


FOLDED = ((0, 0, ROWS), (1, 0, ROWS), (SIDE - 1, 0, ROWS), (2, 0, HALF), (2, ROWS, HALF))


def fold_kernel(tail, panel_in, inverses_in, folded, panel, inverses):
    x = lax.axis_index("front") // SIDE
    top = 0
    for step, first, height in FOLDED:
        at = pl.multiple_of(lax.rem(x + step, SIDE) * LINE, LINE)
        folded[top : top + height, :LINE] = tail[first : first + height, pl.ds(at, LINE)]
        first += height
        folded[top : top + height, LINE:] = tail[first : first + height, pl.ds(at, LINE)]
        top += height
    panel[...] = panel_in[...]
    inverses[...] = inverses_in[...]


def fold_tail(tail, panel, inverses):
    return pl.pallas_call(
        fold_kernel,
        out_shape=(
            jax.ShapeDtypeStruct((SIDE * ROWS, PANEL), jnp.bfloat16),
            jax.ShapeDtypeStruct(panel.shape, jnp.bfloat16),
            jax.ShapeDtypeStruct(inverses.shape, jnp.bfloat16),
        ),
        in_specs=[VMEM_SPEC] * 3,
        out_specs=(VMEM_SPEC,) * 3,
        compiler_params=pltpu.CompilerParams(vmem_limit_bytes=6 * MIB),
        cost_estimate=pl.CostEstimate(flops=0, bytes_accessed=2 * MIB, transcendentals=0),
        name="fold",
    )(tail, panel, inverses)


def message_kernel(folded, panel, low, high, far, up, down):
    for part, out in enumerate((up, down)):
        first = (part + 1) * ROWS
        out[:ROWS] = folded[first : first + ROWS]
        first = 3 * ROWS + part * HALF
        out[LAST:] = folded[first : first + HALF]
    for out, first, second in ((up, ON_AT, MIDDLE), (down, MIDDLE, ON_AT)):
        out[first : first + ROWS] = panel[...]
        out[first + ROWS : first + 2 * ROWS] = low[...]
        out[second : second + ROWS] = high[...]
        out[second + ROWS : second + 2 * ROWS] = far[...]


def make_messages(folded, panels):
    message = jax.ShapeDtypeStruct((MESSAGE, PANEL), jnp.bfloat16)
    return pl.pallas_call(
        message_kernel,
        out_shape=(message, message),
        in_specs=[VMEM_SPEC] * 5,
        out_specs=(VMEM_SPEC,) * 2,
        compiler_params=pltpu.CompilerParams(vmem_limit_bytes=6 * MIB),
        cost_estimate=pl.CostEstimate(flops=0, bytes_accessed=2 * MIB, transcendentals=0),
        name="messages",
    )(folded, *panels)


def tile_kernel(chunk, sizes, rows_x, rows_z, *refs):
    (kept, left, right, ahead, behind), (out, product, tails, rows) = refs[:5], refs[5:]
    front = lax.axis_index("front")
    live = sizes[lax.axis_index("leaf")]
    x, z = front // SIDE, lax.rem(front, SIDE)
    lane = lax.broadcasted_iota(jnp.int32, (BLOCK, BLOCK), 1)
    line = lax.broadcasted_iota(jnp.int32, (BLOCK, BLOCK), 0)
    for step, source in ((0, kept), (1, left), (SIDE - 1, right)):
        tails[step, :ROWS] = source[:ROWS, :LINE]
        tails[step, ROWS:] = source[:ROWS, LINE:]
    for part, source in enumerate((ahead, behind)):
        first = part * ROWS
        tails[2, first : first + HALF] = source[2 * ROWS :, :LINE]
        tails[2, first + HALF : first + ROWS] = source[2 * ROWS :, LINE:]
    for up, row_x in enumerate(chunk):
        away = lax.rem(row_x - x + SIDE, SIDE)
        at = jnp.where(away == 0, 0, jnp.where(away == SIDE - 1, 1, away + 1))
        at = pl.multiple_of(at * BLOCK, BLOCK)
        rows[up * BLOCK : (up + 1) * BLOCK, :] = rows_x[pl.ds(at, BLOCK), :]
    for at in range(0, LINE, WIDE):
        product[:, at : at + WIDE] = dot_nt(rows[...], rows_z[at : at + WIDE, :])
    for up, row_x in enumerate(chunk):
        step = lax.rem(x - row_x + SIDE, SIDE)
        for across, dz in enumerate(RING):
            col_z = lax.rem(z + dz + SIDE, SIDE)
            columns = slice(across * BLOCK, (across + 1) * BLOCK)
            keep = (line + (row_x * SIDE + z) * BLOCK < live) & (
                lane + (x * SIDE + col_z) * BLOCK < live
            )
            old = tails[step, :, pl.ds(pl.multiple_of(col_z * BLOCK, BLOCK), BLOCK)]
            schur = old.astype(jnp.float32) - product[up * BLOCK : (up + 1) * BLOCK, columns]
            out[up * BLOCK : (up + 1) * BLOCK, columns] = jnp.where(keep, schur, 0.0).astype(
                jnp.bfloat16
            )


def make_tile(chunk, sizes, rows_x, rows_z, tails):
    rows = len(chunk) * BLOCK
    return pl.pallas_call(
        functools.partial(tile_kernel, chunk),
        out_shape=jax.ShapeDtypeStruct((rows, LINE), jnp.bfloat16),
        in_specs=[SMEM_SPEC] + [VMEM_SPEC] * 7,
        out_specs=VMEM_SPEC,
        scratch_shapes=[
            pltpu.VMEM((rows, LINE), jnp.float32),
            pltpu.VMEM((SIDE, BLOCK, LINE), jnp.bfloat16),
            pltpu.VMEM((rows, 2 * PANEL), jnp.bfloat16),
        ],
        compiler_params=pltpu.CompilerParams(vmem_limit_bytes=8 * MIB),
        cost_estimate=pl.CostEstimate(
            flops=4 * rows * LINE * PANEL, bytes_accessed=5 * MIB, transcendentals=0
        ),
        name="tile",
    )(sizes, rows_x, rows_z, *tails)


def pack_kernel(plan, line, out):
    rows = line.shape[0] // SIDE
    for at in range(FRONT):

        @pl.when(plan[at] >= 0)
        def _():
            up, across = at // SIDE, at % SIDE
            out[plan[at]] = line[
                up * rows : (up + 1) * rows, across * BLOCK : (across + 1) * BLOCK
            ]


def pack_tiles(plan, line):
    rows = line.shape[0] // SIDE
    return pl.pallas_call(
        pack_kernel,
        out_shape=jax.ShapeDtypeStruct((SIDE * SLOTS, rows, BLOCK), jnp.bfloat16),
        in_specs=[SMEM_SPEC, VMEM_SPEC],
        out_specs=VMEM_SPEC,
        compiler_params=pltpu.CompilerParams(vmem_limit_bytes=4 * MIB),
        cost_estimate=pl.CostEstimate(flops=0, bytes_accessed=6 * MIB, transcendentals=0),
        name="pack",
    )(plan, line)


def blank_kernel(block_map, block_owner, out, plan, blank, taken, sem):
    parent, child, front = family()
    x, z = front // SIDE, lax.rem(front, SIDE)
    blank[...] = jnp.zeros_like(blank)

    @pl.loop(0, 2 * FRONT)
    def _(block):
        taken[block] = 0
        plan[block] = 0

    @pl.loop(0, FRONT)
    def _(block):
        into = block_map[child, block]
        taken[into] = 1
        slot = block_owner[parent, into]

        @pl.when(slot // SLOTS == front)
        def _():
            plan[FRONT + lax.rem(slot, SLOTS)] = 1

    def copy(block):
        row = pl.multiple_of(block * BLOCK, BLOCK)
        return pltpu.make_async_copy(blank, out.at[pl.ds(row, BLOCK), :], sem)

    @pl.loop(0, 2 * FRONT)
    def _(block):
        @pl.when(taken[block] == 0)
        def _():
            copy(block).start()

    for up, dx in enumerate(RING):
        for across, dz in enumerate(RING):
            slot = block_owner[parent, block_map[child, place_of(front, dx, dz)]]
            owner = slot // SLOTS
            step = lax.rem(lax.rem(owner, SIDE) - z + SIDE, SIDE)
            plan[up * SIDE + across] = jnp.where(
                owner // SIDE == x, step * SLOTS + lax.rem(slot, SLOTS), -1
            )

    @pl.loop(0, FRONT)
    def _(block):
        copy(0).wait()


PARENT = jax.ShapeDtypeStruct((2 * CONTRIB, SLOTS * BLOCK), jnp.float32)


def blank_rows(block_map, block_owner):
    return pl.pallas_call(
        blank_kernel,
        out_shape=(PARENT, jax.ShapeDtypeStruct((2 * FRONT,), jnp.int32)),
        in_specs=[SMEM_SPEC] * 2,
        out_specs=(HELD, SMEM_SPEC),
        scratch_shapes=[
            pltpu.VMEM((BLOCK, SLOTS * BLOCK), jnp.float32),
            pltpu.SMEM((2 * FRONT,), jnp.int32),
            pltpu.SemaphoreType.DMA,
        ],
        compiler_params=pltpu.CompilerParams(vmem_limit_bytes=2 * MIB),
        cost_estimate=pl.CostEstimate(flops=0, bytes_accessed=3 * MIB, transcendentals=0),
        name="blank",
    )(block_map, block_owner)


def place_kernel(parts, block_map, plan, *refs):
    tiles, (out, staged, sems) = refs[: len(parts)], refs[len(parts) + 1 :]
    _, child, front = family()
    none = lax.broadcasted_iota(jnp.int32, (BLOCK, BLOCK), 0) * 0
    copies = []
    for (chunk, step), tile in zip(parts, tiles, strict=True):
        z = lax.rem(lax.rem(front, SIDE) - step + SIDE, SIDE)
        for up, row_x in enumerate(chunk):
            here = len(copies)
            for slot in range(SLOTS):
                value = tile[slot, up * BLOCK : (up + 1) * BLOCK, :].astype(jnp.float32)
                staged[here, :, slot * BLOCK : (slot + 1) * BLOCK] = jnp.where(
                    none + plan[FRONT + slot] > 0, value, 0.0
                )
            row = pl.multiple_of(block_map[child, row_x * SIDE + z] * BLOCK, BLOCK)
            copy = pltpu.make_async_copy(
                staged.at[here], out.at[pl.ds(row, BLOCK), :], sems.at[here]
            )
            copy.start()
            copies.append(copy)
    for copy in copies:
        copy.wait()


def place_tiles(block_map, plan, parent_rows, tiles):
    blocks = sum(len(chunk) for chunk, _ in tiles)
    return pl.pallas_call(
        functools.partial(place_kernel, list(tiles)),
        out_shape=PARENT,
        in_specs=[SMEM_SPEC] * 2 + [VMEM_SPEC] * len(tiles) + [HELD],
        out_specs=HELD,
        scratch_shapes=[
            pltpu.VMEM((blocks, BLOCK, SLOTS * BLOCK), jnp.float32),
            pltpu.SemaphoreType.DMA((blocks,)),
        ],
        input_output_aliases={2 + len(tiles): 0},
        compiler_params=pltpu.CompilerParams(vmem_limit_bytes=6 * MIB),
        cost_estimate=pl.CostEstimate(flops=0, bytes_accessed=MIB, transcendentals=0),
        name="place",
    )(block_map, plan, *tiles.values(), parent_rows)


def per_device(inv_factors, panel_rows, border, tail, front_sizes, block_map, block_owner):
    inverses, panel = inv_factors[0].reshape(2 * ROWS, PANEL), panel_rows[0]
    left, right = shift(inverses, "x", 1), shift(inverses, "x", -1)
    low, high, far = (shift(panel, "z", -step) for step in RING[1:])
    folded, panel, inverses = fold_tail(tail[0], panel, inverses)
    left, right, folded, panel, inverses = lax.optimization_barrier(
        (left, right, folded, panel, inverses)
    )
    far_first = shift(left[:ROWS], "x", 1)
    far_second = shift(right[ROWS:], "x", -1)

    chunks = lower_chunks(inverses, left, right, far_first, far_second)
    chunks, update, plan = spread(chunks, "z", *blank_rows(block_map, block_owner))
    up, down = make_messages(folded, (panel, low, high, far))
    from_left, from_right = shift(up, "x", 1), shift(down, "x", -1)
    ahead = shift(from_left[ON_AT:], "x", 1)
    behind = shift(from_right[ON_AT:], "x", -1)
    panels = (down, from_left, from_right, ahead, behind)
    link_local, factor_local = eliminate(border[0], chunks, panels)

    rows_x, rows_z = bundle_of(factor_local, "x"), bundle_of(factor_local, "z")
    rows_x, rows_z = lax.optimization_barrier((rows_x, rows_z))
    factor_local = rows_z[:BLOCK]
    tails = (folded, from_left, from_right, ahead, behind)

    tiles = {}
    for chunk in CHUNKS_OF_ROWS:
        rows = make_tile(chunk, front_sizes, rows_x, rows_z, tails)
        there = to_parent(rows)
        if chunk is FIRST:
            there, factor_local = lax.optimization_barrier((there, factor_local))
        packed = pack_tiles(plan, bundle_of(there, "x"))
        for step in range(SIDE):
            tile = packed[step * SLOTS : (step + 1) * SLOTS]
            tiles[chunk, step] = shift(tile, "z", step) if step else tile
    for group in GROUPS:
        update = place_tiles(block_map, plan, update, {key: tiles[key] for key in group})
    return link_local[None], factor_local[None], update[None]


def solution(mesh):
    return jax.shard_map(
        per_device,
        mesh=mesh,
        in_specs=(
            P("leaf", None, "front", None),
            P("leaf", "front", None),
            P("leaf", "front", None),
            P("leaf", "front", None),
            P(),
            P(),
            P(),
        ),
        out_specs=(P("leaf", "front", None), P("leaf", "front", None), P("leaf", None, "front")),
        check_vma=False,
    )
```

```python
import functools

import jax
import jax.numpy as jnp
from jax import lax
from jax.experimental import pallas as pl
from jax.experimental.pallas import tpu as pltpu
from jax.sharding import PartitionSpec as P

PANEL = 1024
BLOCK = 128
SLOTS = 3
SIDE = 4
FRONT = SIDE * SIDE
CONTRIB = BLOCK * FRONT
ROWS = PANEL // FRONT
MIB = 1024 * 1024


def dot_nt(left, right):
    return lax.dot_general(
        left, right, (((1,), (1,)), ((), ())), preferred_element_type=jnp.float32
    )


def shift(value, axis, by):
    dx, dz = (by, 0) if axis == "x" else (0, by)
    pairs = [
        (x * SIDE + z, (x + dx) % SIDE * SIDE + (z + dz) % SIDE)
        for x in range(SIDE)
        for z in range(SIDE)
    ]
    return lax.ppermute(value, "front", pairs)


def to_parent(value):
    groups = lax.axis_size("leaf")
    return lax.ppermute(
        value, "leaf", [(g, (g + groups // 2) % groups) for g in range(groups)]
    )


RING = (0, -1, 1, 2)


def bundle_of(own, axis):
    half = own.shape[0] // 2
    from_left = shift(own, axis, 1)
    from_right = shift(own, axis, -1)
    far_top = shift(from_left[:half], axis, 1)
    far_bottom = shift(from_right[half:], axis, -1)
    return jnp.concatenate([own, from_left, from_right, far_top, far_bottom], axis=0)


def direct_bundle(own, axis):
    return jnp.concatenate([own] + [shift(own, axis, -step) for step in RING[1:]], axis=0)


def spread(bundle, axis, *meanwhile):
    half = bundle.shape[0] // 2
    left = shift(bundle, axis, 1)
    right = shift(bundle, axis, -1)
    left, right, meanwhile = lax.optimization_barrier((left, right, meanwhile))
    far_low = shift(left[:half], axis, 1)
    far_high = shift(right[half:], axis, -1)
    return [bundle, left, right, far_low, far_high], *meanwhile


def places(x_first):
    found = []
    for part, second in ((RING, 0), (RING, -1), (RING, 1), (RING[:2], 2), (RING[2:], 2)):
        found.append([(first, second) if x_first else (second, first) for first in part])
    return found


X_FIRST, Z_FIRST = places(True), places(False)


def place_of(front, dx, dz):
    x, z = front // SIDE, front % SIDE
    return lax.rem(x + dx + SIDE, SIDE) * SIDE + lax.rem(z + dz + SIDE, SIDE)


def family():
    groups = lax.axis_size("leaf")
    parent = lax.axis_index("leaf")
    return parent, lax.rem(parent + groups // 2, groups), lax.axis_index("front")


def unpack_inverses(front, bundles, mats):
    z = lax.rem(front, SIDE)
    for bundle, dz, start in zip(bundles, (0, -1, 1, 2, 2), (0, 0, 0, 0, CHUNKS // 2), strict=True):
        place = lax.rem(z + dz + SIDE, SIDE) * ROWS
        for at in range(bundle.shape[0] // (2 * ROWS)):
            x, chunk = LOWER[start + at]
            row = pl.multiple_of(place + x * SIDE * ROWS, ROWS)
            for which in range(2):
                top = (at * 2 + which) * ROWS
                mats[which, pl.ds(row, ROWS), chunk * WIDE : (chunk + 1) * WIDE] = bundle[
                    top : top + ROWS, :
                ]


def unpack_panel(front, sources, mat):
    own, left, right, ahead, behind = sources
    half = 2 * ROWS
    parts = [(own, MIDDLE, 0, 0), (own, ON_AT, 1, 0), (left, ON_AT, 0, -1), (left, MIDDLE, 1, -1)]
    parts += [(right, MIDDLE, 0, 1), (right, ON_AT, 1, 1), (ahead, 0, 0, 2), (behind, 0, 1, 2)]
    for source, top, part, dx in parts:
        for at, dz in enumerate(RING[part * 2 : part * 2 + 2]):
            row = pl.multiple_of(place_of(front, dx, dz) * ROWS, ROWS)
            first = top + at * half // 2
            mat[pl.ds(row, ROWS), :] = source[first : first + ROWS, :]


WIDE = SIDE * ROWS
TALL = 576
LOWER = [(x, chunk) for x in range(SIDE) for chunk in range(x + 1)]
CHUNKS = len(LOWER)


def project(rows, inverse, keep):
    for at in range(0, PANEL, WIDE):
        upto = at + WIDE
        keep(at, dot_nt(rows[:, :upto], inverse[at:upto, :upto]))


def lower_kernel(*refs):
    sources, out = refs[:5], refs[5]
    x = lax.axis_index("front") // SIDE
    blocks = [(sources[0], 0, 0), (sources[1], 0, -1), (sources[2], 0, 1)]
    blocks += [(sources[3], 0, 2), (sources[4], 1, 2)]
    for source, first, dx in blocks:
        from_x = lax.rem(x + dx + SIDE, SIDE)
        start = (from_x * (from_x + 1)) // 2
        for chunk in range(SIDE):

            @pl.when(chunk <= from_x)
            def _():
                row = pl.multiple_of((start + chunk) * 2 * ROWS + first * ROWS, ROWS)
                out[pl.ds(row, source.shape[0]), :] = source[:, chunk * WIDE : (chunk + 1) * WIDE]


def lower_chunks(own, left, right, far_first, far_second):
    return pl.pallas_call(
        lower_kernel,
        out_shape=jax.ShapeDtypeStruct((CHUNKS * 2 * ROWS, WIDE), jnp.bfloat16),
        in_specs=[VMEM_SPEC] * 5,
        out_specs=VMEM_SPEC,
        compiler_params=pltpu.CompilerParams(vmem_limit_bytes=4 * MIB),
        cost_estimate=pl.CostEstimate(flops=0, bytes_accessed=MIB, transcendentals=0),
        name="lower",
    )(own, left, right, far_first, far_second)


def panel_kernel(border, *refs):
    inverses, panels, (link_out, factor) = refs[:5], refs[5:10], refs[10:12]
    mats, both, link, updated = refs[12:]
    front = lax.axis_index("front")
    unpack_inverses(front, inverses, mats)

    both[:BLOCK] = border[:, :PANEL]
    unpack_panel(front, panels, both.at[BLOCK:])

    def keep_both(up):
        def keep(at, value):
            if up == 0:
                factor[:, at : at + WIDE] = value[:BLOCK].astype(jnp.bfloat16)
                value = value[BLOCK:]
            first = max(up - BLOCK, 0)
            link[first : first + value.shape[0], at : at + WIDE] = value.astype(jnp.bfloat16)

        return keep

    def keep_second(at, value):
        factor[:, PANEL + at : PANEL + at + WIDE] = value.astype(jnp.bfloat16)

    for up in range(0, BLOCK + PANEL, TALL):
        project(both.at[up : up + TALL], mats.at[0], keep_both(up))
    link_out[...] = link[pl.ds(pl.multiple_of(front * ROWS, ROWS), ROWS), :]
    for at in range(0, PANEL, WIDE):
        coupled = dot_nt(factor[:, :PANEL], link[at : at + WIDE, :])
        updated[:, at : at + WIDE] = (
            border[:, PANEL + at : PANEL + at + WIDE].astype(jnp.float32) - coupled
        ).astype(jnp.bfloat16)
    project(updated, mats.at[1], keep_second)


VMEM_SPEC = pl.BlockSpec(memory_space=pltpu.VMEM)
SMEM_SPEC = pl.BlockSpec(memory_space=pltpu.SMEM)
HELD = pl.BlockSpec(memory_space=pl.ANY)


def eliminate(border, inverses, panels):
    return pl.pallas_call(
        panel_kernel,
        out_shape=(
            jax.ShapeDtypeStruct((ROWS, PANEL), jnp.bfloat16),
            jax.ShapeDtypeStruct((BLOCK, 2 * PANEL), jnp.bfloat16),
        ),
        in_specs=[VMEM_SPEC] * 11,
        out_specs=(VMEM_SPEC,) * 2,
        scratch_shapes=[
            pltpu.VMEM((2, PANEL, PANEL), jnp.bfloat16),
            pltpu.VMEM((BLOCK + PANEL, PANEL), jnp.bfloat16),
            pltpu.VMEM((PANEL, PANEL), jnp.bfloat16),
            pltpu.VMEM((BLOCK, PANEL), jnp.bfloat16),
        ],
        compiler_params=pltpu.CompilerParams(vmem_limit_bytes=16 * MIB),
        cost_estimate=pl.CostEstimate(
            flops=2 * PANEL**3 + 6 * BLOCK * PANEL**2,
            bytes_accessed=8 * MIB,
            transcendentals=0,
        ),
        name="panels",
    )(border, *inverses, *panels)


LINE = SIDE * BLOCK
CHUNKS_OF_ROWS = ((0, 1), (2, 3))
FIRST, SECOND = CHUNKS_OF_ROWS
GROUPS = (
    [(FIRST, step) for step in range(SIDE)] + [(SECOND, 0)],
    [(SECOND, step) for step in range(1, SIDE)],
)
HALF = ROWS // 2
MIDDLE, ON_AT, LAST, MESSAGE = ROWS, 3 * ROWS, 5 * ROWS, 5 * ROWS + HALF


FOLDED = ((0, 0, ROWS), (1, 0, ROWS), (SIDE - 1, 0, ROWS), (2, 0, HALF), (2, ROWS, HALF))


def fold_kernel(tail, panel_in, inverses_in, folded, panel, inverses):
    x = lax.axis_index("front") // SIDE
    top = 0
    for step, first, height in FOLDED:
        at = pl.multiple_of(lax.rem(x + step, SIDE) * LINE, LINE)
        folded[top : top + height, :LINE] = tail[first : first + height, pl.ds(at, LINE)]
        first += height
        folded[top : top + height, LINE:] = tail[first : first + height, pl.ds(at, LINE)]
        top += height
    panel[...] = panel_in[...]
    inverses[...] = inverses_in[...]


def fold_tail(tail, panel, inverses):
    return pl.pallas_call(
        fold_kernel,
        out_shape=(
            jax.ShapeDtypeStruct((SIDE * ROWS, PANEL), jnp.bfloat16),
            jax.ShapeDtypeStruct(panel.shape, jnp.bfloat16),
            jax.ShapeDtypeStruct(inverses.shape, jnp.bfloat16),
        ),
        in_specs=[VMEM_SPEC] * 3,
        out_specs=(VMEM_SPEC,) * 3,
        compiler_params=pltpu.CompilerParams(vmem_limit_bytes=6 * MIB),
        cost_estimate=pl.CostEstimate(flops=0, bytes_accessed=2 * MIB, transcendentals=0),
        name="fold",
    )(tail, panel, inverses)


def message_kernel(folded, panel, low, high, far, up, down):
    for part, out in enumerate((up, down)):
        first = (part + 1) * ROWS
        out[:ROWS] = folded[first : first + ROWS]
        first = 3 * ROWS + part * HALF
        out[LAST:] = folded[first : first + HALF]
    for out, first, second in ((up, ON_AT, MIDDLE), (down, MIDDLE, ON_AT)):
        out[first : first + ROWS] = panel[...]
        out[first + ROWS : first + 2 * ROWS] = low[...]
        out[second : second + ROWS] = high[...]
        out[second + ROWS : second + 2 * ROWS] = far[...]


def make_messages(folded, panels):
    message = jax.ShapeDtypeStruct((MESSAGE, PANEL), jnp.bfloat16)
    return pl.pallas_call(
        message_kernel,
        out_shape=(message, message),
        in_specs=[VMEM_SPEC] * 5,
        out_specs=(VMEM_SPEC,) * 2,
        compiler_params=pltpu.CompilerParams(vmem_limit_bytes=6 * MIB),
        cost_estimate=pl.CostEstimate(flops=0, bytes_accessed=2 * MIB, transcendentals=0),
        name="messages",
    )(folded, *panels)


def tile_kernel(chunk, sizes, rows_x, rows_z, *refs):
    (kept, left, right, ahead, behind), (out, product, tails, rows) = refs[:5], refs[5:]
    front = lax.axis_index("front")
    live = sizes[lax.axis_index("leaf")]
    x, z = front // SIDE, lax.rem(front, SIDE)
    lane = lax.broadcasted_iota(jnp.int32, (BLOCK, BLOCK), 1)
    line = lax.broadcasted_iota(jnp.int32, (BLOCK, BLOCK), 0)
    for step, source in ((0, kept), (1, left), (SIDE - 1, right)):
        tails[step, :ROWS] = source[:ROWS, :LINE]
        tails[step, ROWS:] = source[:ROWS, LINE:]
    for part, source in enumerate((ahead, behind)):
        first = part * ROWS
        tails[2, first : first + HALF] = source[2 * ROWS :, :LINE]
        tails[2, first + HALF : first + ROWS] = source[2 * ROWS :, LINE:]
    for up, row_x in enumerate(chunk):
        away = lax.rem(row_x - x + SIDE, SIDE)
        at = jnp.where(away == 0, 0, jnp.where(away == SIDE - 1, 1, away + 1))
        at = pl.multiple_of(at * BLOCK, BLOCK)
        rows[up * BLOCK : (up + 1) * BLOCK, :] = rows_x[pl.ds(at, BLOCK), :]
    for at in range(0, LINE, WIDE):
        product[:, at : at + WIDE] = dot_nt(rows[...], rows_z[at : at + WIDE, :])
    for up, row_x in enumerate(chunk):
        step = lax.rem(x - row_x + SIDE, SIDE)
        for across, dz in enumerate(RING):
            col_z = lax.rem(z + dz + SIDE, SIDE)
            columns = slice(across * BLOCK, (across + 1) * BLOCK)
            keep = (line + (row_x * SIDE + z) * BLOCK < live) & (
                lane + (x * SIDE + col_z) * BLOCK < live
            )
            old = tails[step, :, pl.ds(pl.multiple_of(col_z * BLOCK, BLOCK), BLOCK)]
            schur = old.astype(jnp.float32) - product[up * BLOCK : (up + 1) * BLOCK, columns]
            out[up * BLOCK : (up + 1) * BLOCK, columns] = jnp.where(keep, schur, 0.0).astype(
                jnp.bfloat16
            )


def make_tile(chunk, sizes, rows_x, rows_z, tails):
    rows = len(chunk) * BLOCK
    return pl.pallas_call(
        functools.partial(tile_kernel, chunk),
        out_shape=jax.ShapeDtypeStruct((rows, LINE), jnp.bfloat16),
        in_specs=[SMEM_SPEC] + [VMEM_SPEC] * 7,
        out_specs=VMEM_SPEC,
        scratch_shapes=[
            pltpu.VMEM((rows, LINE), jnp.float32),
            pltpu.VMEM((SIDE, BLOCK, LINE), jnp.bfloat16),
            pltpu.VMEM((rows, 2 * PANEL), jnp.bfloat16),
        ],
        compiler_params=pltpu.CompilerParams(vmem_limit_bytes=8 * MIB),
        cost_estimate=pl.CostEstimate(
            flops=4 * rows * LINE * PANEL, bytes_accessed=5 * MIB, transcendentals=0
        ),
        name="tile",
    )(sizes, rows_x, rows_z, *tails)


def pack_kernel(plan, line, out):
    rows = line.shape[0] // SIDE
    for at in range(FRONT):

        @pl.when(plan[at] >= 0)
        def _():
            up, across = at // SIDE, at % SIDE
            out[plan[at]] = line[
                up * rows : (up + 1) * rows, across * BLOCK : (across + 1) * BLOCK
            ]


def pack_tiles(plan, line):
    rows = line.shape[0] // SIDE
    return pl.pallas_call(
        pack_kernel,
        out_shape=jax.ShapeDtypeStruct((SIDE * SLOTS, rows, BLOCK), jnp.bfloat16),
        in_specs=[SMEM_SPEC, VMEM_SPEC],
        out_specs=VMEM_SPEC,
        compiler_params=pltpu.CompilerParams(vmem_limit_bytes=4 * MIB),
        cost_estimate=pl.CostEstimate(flops=0, bytes_accessed=6 * MIB, transcendentals=0),
        name="pack",
    )(plan, line)


def blank_kernel(block_map, block_owner, out, plan, blank, taken, sem):
    parent, child, front = family()
    x, z = front // SIDE, lax.rem(front, SIDE)
    blank[...] = jnp.zeros_like(blank)

    @pl.loop(0, 2 * FRONT)
    def _(block):
        taken[block] = 0
        plan[block] = 0

    @pl.loop(0, FRONT)
    def _(block):
        into = block_map[child, block]
        taken[into] = 1
        slot = block_owner[parent, into]

        @pl.when(slot // SLOTS == front)
        def _():
            plan[FRONT + lax.rem(slot, SLOTS)] = 1

    def copy(block):
        row = pl.multiple_of(block * BLOCK, BLOCK)
        return pltpu.make_async_copy(blank, out.at[pl.ds(row, BLOCK), :], sem)

    @pl.loop(0, 2 * FRONT)
    def _(block):
        @pl.when(taken[block] == 0)
        def _():
            copy(block).start()

    for up, dx in enumerate(RING):
        for across, dz in enumerate(RING):
            slot = block_owner[parent, block_map[child, place_of(front, dx, dz)]]
            owner = slot // SLOTS
            step = lax.rem(lax.rem(owner, SIDE) - z + SIDE, SIDE)
            plan[up * SIDE + across] = jnp.where(
                owner // SIDE == x, step * SLOTS + lax.rem(slot, SLOTS), -1
            )

    @pl.loop(0, FRONT)
    def _(block):
        copy(0).wait()


PARENT = jax.ShapeDtypeStruct((2 * CONTRIB, SLOTS * BLOCK), jnp.float32)


def blank_rows(block_map, block_owner):
    return pl.pallas_call(
        blank_kernel,
        out_shape=(PARENT, jax.ShapeDtypeStruct((2 * FRONT,), jnp.int32)),
        in_specs=[SMEM_SPEC] * 2,
        out_specs=(HELD, SMEM_SPEC),
        scratch_shapes=[
            pltpu.VMEM((BLOCK, SLOTS * BLOCK), jnp.float32),
            pltpu.SMEM((2 * FRONT,), jnp.int32),
            pltpu.SemaphoreType.DMA,
        ],
        compiler_params=pltpu.CompilerParams(vmem_limit_bytes=2 * MIB),
        cost_estimate=pl.CostEstimate(flops=0, bytes_accessed=3 * MIB, transcendentals=0),
        name="blank",
    )(block_map, block_owner)


def place_kernel(parts, block_map, plan, *refs):
    tiles, (out, staged, sems) = refs[: len(parts)], refs[len(parts) + 1 :]
    _, child, front = family()
    none = lax.broadcasted_iota(jnp.int32, (BLOCK, BLOCK), 0) * 0
    copies = []
    for (chunk, step), tile in zip(parts, tiles, strict=True):
        z = lax.rem(lax.rem(front, SIDE) - step + SIDE, SIDE)
        for up, row_x in enumerate(chunk):
            here = len(copies)
            for slot in range(SLOTS):
                value = tile[slot, up * BLOCK : (up + 1) * BLOCK, :].astype(jnp.float32)
                staged[here, :, slot * BLOCK : (slot + 1) * BLOCK] = jnp.where(
                    none + plan[FRONT + slot] > 0, value, 0.0
                )
            row = pl.multiple_of(block_map[child, row_x * SIDE + z] * BLOCK, BLOCK)
            copy = pltpu.make_async_copy(
                staged.at[here], out.at[pl.ds(row, BLOCK), :], sems.at[here]
            )
            copy.start()
            copies.append(copy)
    for copy in copies:
        copy.wait()


def place_tiles(block_map, plan, parent_rows, tiles):
    blocks = sum(len(chunk) for chunk, _ in tiles)
    return pl.pallas_call(
        functools.partial(place_kernel, list(tiles)),
        out_shape=PARENT,
        in_specs=[SMEM_SPEC] * 2 + [VMEM_SPEC] * len(tiles) + [HELD],
        out_specs=HELD,
        scratch_shapes=[
            pltpu.VMEM((blocks, BLOCK, SLOTS * BLOCK), jnp.float32),
            pltpu.SemaphoreType.DMA((blocks,)),
        ],
        input_output_aliases={2 + len(tiles): 0},
        compiler_params=pltpu.CompilerParams(vmem_limit_bytes=6 * MIB),
        cost_estimate=pl.CostEstimate(flops=0, bytes_accessed=MIB, transcendentals=0),
        name="place",
    )(block_map, plan, *tiles.values(), parent_rows)


def per_device(inv_factors, panel_rows, border, tail, front_sizes, block_map, block_owner):
    inverses, panel = inv_factors[0].reshape(2 * ROWS, PANEL), panel_rows[0]
    left, right = shift(inverses, "x", 1), shift(inverses, "x", -1)
    low, high, far = (shift(panel, "z", -step) for step in RING[1:])
    folded, panel, inverses = fold_tail(tail[0], panel, inverses)
    left, right, folded, panel, inverses = lax.optimization_barrier(
        (left, right, folded, panel, inverses)
    )
    far_first = shift(left[:ROWS], "x", 1)
    far_second = shift(right[ROWS:], "x", -1)

    chunks = lower_chunks(inverses, left, right, far_first, far_second)
    chunks, update, plan = spread(chunks, "z", *blank_rows(block_map, block_owner))
    up, down = make_messages(folded, (panel, low, high, far))
    from_left, from_right = shift(up, "x", 1), shift(down, "x", -1)
    ahead = shift(from_left[ON_AT:], "x", 1)
    behind = shift(from_right[ON_AT:], "x", -1)
    panels = (down, from_left, from_right, ahead, behind)
    link_local, factor_local = eliminate(border[0], chunks, panels)

    rows_x, rows_z = bundle_of(factor_local, "x"), bundle_of(factor_local, "z")
    rows_x, rows_z = lax.optimization_barrier((rows_x, rows_z))
    factor_local = rows_z[:BLOCK]
    tails = (folded, from_left, from_right, ahead, behind)

    tiles = {}
    for chunk in CHUNKS_OF_ROWS:
        rows = make_tile(chunk, front_sizes, rows_x, rows_z, tails)
        there = to_parent(rows)
        if chunk is FIRST:
            there, factor_local = lax.optimization_barrier((there, factor_local))
        gather = direct_bundle if chunk is FIRST else bundle_of
        packed = pack_tiles(plan, gather(there, "x"))
        for step in range(SIDE):
            tile = packed[step * SLOTS : (step + 1) * SLOTS]
            tiles[chunk, step] = shift(tile, "z", step) if step else tile
    for group in GROUPS:
        update = place_tiles(block_map, plan, update, {key: tiles[key] for key in group})
    return link_local[None], factor_local[None], update[None]


def solution(mesh):
    return jax.shard_map(
        per_device,
        mesh=mesh,
        in_specs=(
            P("leaf", None, "front", None),
            P("leaf", "front", None),
            P("leaf", "front", None),
            P("leaf", "front", None),
            P(),
            P(),
            P(),
        ),
        out_specs=(P("leaf", "front", None), P("leaf", "front", None), P("leaf", None, "front")),
        check_vma=False,
    )
```

```python
import functools

import jax
import jax.numpy as jnp
from jax import lax
from jax.experimental import pallas as pl
from jax.experimental.pallas import tpu as pltpu
from jax.sharding import PartitionSpec as P

PANEL = 1024
BLOCK = 128
SLOTS = 3
SIDE = 4
FRONT = SIDE * SIDE
CONTRIB = BLOCK * FRONT
ROWS = PANEL // FRONT
MIB = 1024 * 1024


def dot_nt(left, right):
    return lax.dot_general(
        left, right, (((1,), (1,)), ((), ())), preferred_element_type=jnp.float32
    )


def shift(value, axis, by):
    dx, dz = (by, 0) if axis == "x" else (0, by)
    pairs = [
        (x * SIDE + z, (x + dx) % SIDE * SIDE + (z + dz) % SIDE)
        for x in range(SIDE)
        for z in range(SIDE)
    ]
    return lax.ppermute(value, "front", pairs)


def to_parent(value):
    groups = lax.axis_size("leaf")
    return lax.ppermute(
        value, "leaf", [(g, (g + groups // 2) % groups) for g in range(groups)]
    )


RING = (0, -1, 1, 2)


def bundle_of(own, axis):
    half = own.shape[0] // 2
    from_left = shift(own, axis, 1)
    from_right = shift(own, axis, -1)
    far_top = shift(from_left[:half], axis, 1)
    far_bottom = shift(from_right[half:], axis, -1)
    return jnp.concatenate([own, from_left, from_right, far_top, far_bottom], axis=0)


def direct_bundle(own, axis):
    return jnp.concatenate([own] + [shift(own, axis, -step) for step in RING[1:]], axis=0)


def spread(bundle, axis, *meanwhile):
    half = bundle.shape[0] // 2
    left = shift(bundle, axis, 1)
    right = shift(bundle, axis, -1)
    left, right, meanwhile = lax.optimization_barrier((left, right, meanwhile))
    far_low = shift(left[:half], axis, 1)
    far_high = shift(right[half:], axis, -1)
    return [bundle, left, right, far_low, far_high], *meanwhile


def places(x_first):
    found = []
    for part, second in ((RING, 0), (RING, -1), (RING, 1), (RING[:2], 2), (RING[2:], 2)):
        found.append([(first, second) if x_first else (second, first) for first in part])
    return found


X_FIRST, Z_FIRST = places(True), places(False)


def place_of(front, dx, dz):
    x, z = front // SIDE, front % SIDE
    return lax.rem(x + dx + SIDE, SIDE) * SIDE + lax.rem(z + dz + SIDE, SIDE)


def family():
    groups = lax.axis_size("leaf")
    parent = lax.axis_index("leaf")
    return parent, lax.rem(parent + groups // 2, groups), lax.axis_index("front")


def unpack_inverses(front, bundles, mats):
    z = lax.rem(front, SIDE)
    for bundle, dz, start in zip(bundles, (0, -1, 1, 2, 2), (0, 0, 0, 0, CHUNKS // 2), strict=True):
        place = lax.rem(z + dz + SIDE, SIDE) * ROWS
        for at in range(bundle.shape[0] // (2 * ROWS)):
            x, chunk = LOWER[start + at]
            row = pl.multiple_of(place + x * SIDE * ROWS, ROWS)
            for which in range(2):
                top = (at * 2 + which) * ROWS
                mats[which, pl.ds(row, ROWS), chunk * WIDE : (chunk + 1) * WIDE] = bundle[
                    top : top + ROWS, :
                ]


def unpack_panel(front, sources, mat):
    own, left, right, ahead, behind = sources
    half = 2 * ROWS
    parts = [(own, MIDDLE, 0, 0), (own, ON_AT, 1, 0), (left, ON_AT, 0, -1), (left, MIDDLE, 1, -1)]
    parts += [(right, MIDDLE, 0, 1), (right, ON_AT, 1, 1), (ahead, 0, 0, 2), (behind, 0, 1, 2)]
    for source, top, part, dx in parts:
        for at, dz in enumerate(RING[part * 2 : part * 2 + 2]):
            row = pl.multiple_of(place_of(front, dx, dz) * ROWS, ROWS)
            first = top + at * half // 2
            mat[pl.ds(row, ROWS), :] = source[first : first + ROWS, :]


WIDE = SIDE * ROWS
TALL = 576
LOWER = [(x, chunk) for x in range(SIDE) for chunk in range(x + 1)]
CHUNKS = len(LOWER)


def project(rows, inverse, keep):
    for at in range(0, PANEL, WIDE):
        upto = at + WIDE
        keep(at, dot_nt(rows[:, :upto], inverse[at:upto, :upto]))


def lower_kernel(*refs):
    sources, out = refs[:5], refs[5]
    x = lax.axis_index("front") // SIDE
    blocks = [(sources[0], 0, 0), (sources[1], 0, -1), (sources[2], 0, 1)]
    blocks += [(sources[3], 0, 2), (sources[4], 1, 2)]
    for source, first, dx in blocks:
        from_x = lax.rem(x + dx + SIDE, SIDE)
        start = (from_x * (from_x + 1)) // 2
        for chunk in range(SIDE):

            @pl.when(chunk <= from_x)
            def _():
                row = pl.multiple_of((start + chunk) * 2 * ROWS + first * ROWS, ROWS)
                out[pl.ds(row, source.shape[0]), :] = source[:, chunk * WIDE : (chunk + 1) * WIDE]


def lower_chunks(own, left, right, far_first, far_second):
    return pl.pallas_call(
        lower_kernel,
        out_shape=jax.ShapeDtypeStruct((CHUNKS * 2 * ROWS, WIDE), jnp.bfloat16),
        in_specs=[VMEM_SPEC] * 5,
        out_specs=VMEM_SPEC,
        compiler_params=pltpu.CompilerParams(vmem_limit_bytes=4 * MIB),
        cost_estimate=pl.CostEstimate(flops=0, bytes_accessed=MIB, transcendentals=0),
        name="lower",
    )(own, left, right, far_first, far_second)


def panel_kernel(border, *refs):
    inverses, panels, (link_out, factor) = refs[:5], refs[5:10], refs[10:12]
    mats, both, link, updated = refs[12:]
    front = lax.axis_index("front")
    unpack_inverses(front, inverses, mats)

    both[:BLOCK] = border[:, :PANEL]
    unpack_panel(front, panels, both.at[BLOCK:])

    def keep_both(up):
        def keep(at, value):
            if up == 0:
                factor[:, at : at + WIDE] = value[:BLOCK].astype(jnp.bfloat16)
                value = value[BLOCK:]
            first = max(up - BLOCK, 0)
            link[first : first + value.shape[0], at : at + WIDE] = value.astype(jnp.bfloat16)

        return keep

    def keep_second(at, value):
        factor[:, PANEL + at : PANEL + at + WIDE] = value.astype(jnp.bfloat16)

    for up in range(0, BLOCK + PANEL, TALL):
        project(both.at[up : up + TALL], mats.at[0], keep_both(up))
    link_out[...] = link[pl.ds(pl.multiple_of(front * ROWS, ROWS), ROWS), :]
    for at in range(0, PANEL, WIDE):
        coupled = dot_nt(factor[:, :PANEL], link[at : at + WIDE, :])
        updated[:, at : at + WIDE] = (
            border[:, PANEL + at : PANEL + at + WIDE].astype(jnp.float32) - coupled
        ).astype(jnp.bfloat16)
    project(updated, mats.at[1], keep_second)


VMEM_SPEC = pl.BlockSpec(memory_space=pltpu.VMEM)
SMEM_SPEC = pl.BlockSpec(memory_space=pltpu.SMEM)
HELD = pl.BlockSpec(memory_space=pl.ANY)


def eliminate(border, inverses, panels):
    return pl.pallas_call(
        panel_kernel,
        out_shape=(
            jax.ShapeDtypeStruct((ROWS, PANEL), jnp.bfloat16),
            jax.ShapeDtypeStruct((BLOCK, 2 * PANEL), jnp.bfloat16),
        ),
        in_specs=[VMEM_SPEC] * 11,
        out_specs=(VMEM_SPEC,) * 2,
        scratch_shapes=[
            pltpu.VMEM((2, PANEL, PANEL), jnp.bfloat16),
            pltpu.VMEM((BLOCK + PANEL, PANEL), jnp.bfloat16),
            pltpu.VMEM((PANEL, PANEL), jnp.bfloat16),
            pltpu.VMEM((BLOCK, PANEL), jnp.bfloat16),
        ],
        compiler_params=pltpu.CompilerParams(vmem_limit_bytes=16 * MIB),
        cost_estimate=pl.CostEstimate(
            flops=2 * PANEL**3 + 6 * BLOCK * PANEL**2,
            bytes_accessed=8 * MIB,
            transcendentals=0,
        ),
        name="panels",
    )(border, *inverses, *panels)


LINE = SIDE * BLOCK
CHUNKS_OF_ROWS = ((0, 1), (2, 3))
FIRST, SECOND = CHUNKS_OF_ROWS
GROUPS = (
    [(FIRST, step) for step in range(SIDE)] + [(SECOND, 0)],
    [(SECOND, step) for step in range(1, SIDE)],
)
HALF = ROWS // 2
MIDDLE, ON_AT, LAST, MESSAGE = ROWS, 3 * ROWS, 5 * ROWS, 5 * ROWS + HALF


FOLDED = ((0, 0, ROWS), (1, 0, ROWS), (SIDE - 1, 0, ROWS), (2, 0, HALF), (2, ROWS, HALF))


def fold_kernel(tail, panel_in, inverses_in, folded, panel, inverses):
    x = lax.axis_index("front") // SIDE
    top = 0
    for step, first, height in FOLDED:
        at = pl.multiple_of(lax.rem(x + step, SIDE) * LINE, LINE)
        folded[top : top + height, :LINE] = tail[first : first + height, pl.ds(at, LINE)]
        first += height
        folded[top : top + height, LINE:] = tail[first : first + height, pl.ds(at, LINE)]
        top += height
    panel[...] = panel_in[...]
    inverses[...] = inverses_in[...]


def fold_tail(tail, panel, inverses):
    return pl.pallas_call(
        fold_kernel,
        out_shape=(
            jax.ShapeDtypeStruct((SIDE * ROWS, PANEL), jnp.bfloat16),
            jax.ShapeDtypeStruct(panel.shape, jnp.bfloat16),
            jax.ShapeDtypeStruct(inverses.shape, jnp.bfloat16),
        ),
        in_specs=[VMEM_SPEC] * 3,
        out_specs=(VMEM_SPEC,) * 3,
        compiler_params=pltpu.CompilerParams(vmem_limit_bytes=6 * MIB),
        cost_estimate=pl.CostEstimate(flops=0, bytes_accessed=2 * MIB, transcendentals=0),
        name="fold",
    )(tail, panel, inverses)


def message_kernel(folded, panel, low, high, far, up, down):
    for part, out in enumerate((up, down)):
        first = (part + 1) * ROWS
        out[:ROWS] = folded[first : first + ROWS]
        first = 3 * ROWS + part * HALF
        out[LAST:] = folded[first : first + HALF]
    for out, first, second in ((up, ON_AT, MIDDLE), (down, MIDDLE, ON_AT)):
        out[first : first + ROWS] = panel[...]
        out[first + ROWS : first + 2 * ROWS] = low[...]
        out[second : second + ROWS] = high[...]
        out[second + ROWS : second + 2 * ROWS] = far[...]


def make_messages(folded, panels):
    message = jax.ShapeDtypeStruct((MESSAGE, PANEL), jnp.bfloat16)
    return pl.pallas_call(
        message_kernel,
        out_shape=(message, message),
        in_specs=[VMEM_SPEC] * 5,
        out_specs=(VMEM_SPEC,) * 2,
        compiler_params=pltpu.CompilerParams(vmem_limit_bytes=6 * MIB),
        cost_estimate=pl.CostEstimate(flops=0, bytes_accessed=2 * MIB, transcendentals=0),
        name="messages",
    )(folded, *panels)


def tile_kernel(chunk, sizes, rows_x, rows_z, *refs):
    (kept, left, right, ahead, behind), (out, product, tails, rows) = refs[:5], refs[5:]
    front = lax.axis_index("front")
    live = sizes[lax.axis_index("leaf")]
    x, z = front // SIDE, lax.rem(front, SIDE)
    lane = lax.broadcasted_iota(jnp.int32, (BLOCK, BLOCK), 1)
    line = lax.broadcasted_iota(jnp.int32, (BLOCK, BLOCK), 0)
    for step, source in ((0, kept), (1, left), (SIDE - 1, right)):
        tails[step, :ROWS] = source[:ROWS, :LINE]
        tails[step, ROWS:] = source[:ROWS, LINE:]
    for part, source in enumerate((ahead, behind)):
        first = part * ROWS
        tails[2, first : first + HALF] = source[2 * ROWS :, :LINE]
        tails[2, first + HALF : first + ROWS] = source[2 * ROWS :, LINE:]
    for up, row_x in enumerate(chunk):
        away = lax.rem(row_x - x + SIDE, SIDE)
        at = jnp.where(away == 0, 0, jnp.where(away == SIDE - 1, 1, away + 1))
        at = pl.multiple_of(at * BLOCK, BLOCK)
        rows[up * BLOCK : (up + 1) * BLOCK, :] = rows_x[pl.ds(at, BLOCK), :]
    for at in range(0, LINE, WIDE):
        product[:, at : at + WIDE] = dot_nt(rows[...], rows_z[at : at + WIDE, :])
    for up, row_x in enumerate(chunk):
        step = lax.rem(x - row_x + SIDE, SIDE)
        for across, dz in enumerate(RING):
            col_z = lax.rem(z + dz + SIDE, SIDE)
            columns = slice(across * BLOCK, (across + 1) * BLOCK)
            keep = (line + (row_x * SIDE + z) * BLOCK < live) & (
                lane + (x * SIDE + col_z) * BLOCK < live
            )
            old = tails[step, :, pl.ds(pl.multiple_of(col_z * BLOCK, BLOCK), BLOCK)]
            schur = old.astype(jnp.float32) - product[up * BLOCK : (up + 1) * BLOCK, columns]
            out[up * BLOCK : (up + 1) * BLOCK, columns] = jnp.where(keep, schur, 0.0).astype(
                jnp.bfloat16
            )


def make_tile(chunk, sizes, rows_x, rows_z, tails):
    rows = len(chunk) * BLOCK
    return pl.pallas_call(
        functools.partial(tile_kernel, chunk),
        out_shape=jax.ShapeDtypeStruct((rows, LINE), jnp.bfloat16),
        in_specs=[SMEM_SPEC] + [VMEM_SPEC] * 7,
        out_specs=VMEM_SPEC,
        scratch_shapes=[
            pltpu.VMEM((rows, LINE), jnp.float32),
            pltpu.VMEM((SIDE, BLOCK, LINE), jnp.bfloat16),
            pltpu.VMEM((rows, 2 * PANEL), jnp.bfloat16),
        ],
        compiler_params=pltpu.CompilerParams(vmem_limit_bytes=8 * MIB),
        cost_estimate=pl.CostEstimate(
            flops=4 * rows * LINE * PANEL, bytes_accessed=5 * MIB, transcendentals=0
        ),
        name="tile",
    )(sizes, rows_x, rows_z, *tails)


def pack_kernel(plan, line, out):
    rows = line.shape[0] // SIDE
    for at in range(FRONT):

        @pl.when(plan[at] >= 0)
        def _():
            up, across = at // SIDE, at % SIDE
            out[plan[at]] = line[
                up * rows : (up + 1) * rows, across * BLOCK : (across + 1) * BLOCK
            ]


def pack_tiles(plan, line):
    rows = line.shape[0] // SIDE
    return pl.pallas_call(
        pack_kernel,
        out_shape=jax.ShapeDtypeStruct((SIDE * SLOTS, rows, BLOCK), jnp.bfloat16),
        in_specs=[SMEM_SPEC, VMEM_SPEC],
        out_specs=VMEM_SPEC,
        compiler_params=pltpu.CompilerParams(vmem_limit_bytes=4 * MIB),
        cost_estimate=pl.CostEstimate(flops=0, bytes_accessed=6 * MIB, transcendentals=0),
        name="pack",
    )(plan, line)


def blank_kernel(block_map, block_owner, out, plan, blank, taken, sem):
    parent, child, front = family()
    x, z = front // SIDE, lax.rem(front, SIDE)
    blank[...] = jnp.zeros_like(blank)

    @pl.loop(0, 2 * FRONT)
    def _(block):
        taken[block] = 0
        plan[block] = 0

    @pl.loop(0, FRONT)
    def _(block):
        into = block_map[child, block]
        taken[into] = 1
        slot = block_owner[parent, into]

        @pl.when(slot // SLOTS == front)
        def _():
            plan[FRONT + lax.rem(slot, SLOTS)] = 1

    def copy(block):
        row = pl.multiple_of(block * BLOCK, BLOCK)
        return pltpu.make_async_copy(blank, out.at[pl.ds(row, BLOCK), :], sem)

    @pl.loop(0, 2 * FRONT)
    def _(block):
        @pl.when(taken[block] == 0)
        def _():
            copy(block).start()

    for up, dx in enumerate(RING):
        for across, dz in enumerate(RING):
            slot = block_owner[parent, block_map[child, place_of(front, dx, dz)]]
            owner = slot // SLOTS
            step = lax.rem(lax.rem(owner, SIDE) - z + SIDE, SIDE)
            plan[up * SIDE + across] = jnp.where(
                owner // SIDE == x, step * SLOTS + lax.rem(slot, SLOTS), -1
            )

    @pl.loop(0, FRONT)
    def _(block):
        copy(0).wait()


PARENT = jax.ShapeDtypeStruct((2 * CONTRIB, SLOTS * BLOCK), jnp.float32)


def blank_rows(block_map, block_owner):
    return pl.pallas_call(
        blank_kernel,
        out_shape=(PARENT, jax.ShapeDtypeStruct((2 * FRONT,), jnp.int32)),
        in_specs=[SMEM_SPEC] * 2,
        out_specs=(HELD, SMEM_SPEC),
        scratch_shapes=[
            pltpu.VMEM((BLOCK, SLOTS * BLOCK), jnp.float32),
            pltpu.SMEM((2 * FRONT,), jnp.int32),
            pltpu.SemaphoreType.DMA,
        ],
        compiler_params=pltpu.CompilerParams(vmem_limit_bytes=2 * MIB),
        cost_estimate=pl.CostEstimate(flops=0, bytes_accessed=3 * MIB, transcendentals=0),
        name="blank",
    )(block_map, block_owner)


def place_kernel(parts, block_map, plan, *refs):
    tiles, (out, staged, sems) = refs[: len(parts)], refs[len(parts) + 1 :]
    _, child, front = family()
    copies = []
    for (chunk, step), tile in zip(parts, tiles, strict=True):
        z = lax.rem(lax.rem(front, SIDE) - step + SIDE, SIDE)
        for up, row_x in enumerate(chunk):
            here = len(copies)
            for slot in range(SLOTS):
                columns = slice(slot * BLOCK, (slot + 1) * BLOCK)

                @pl.when(plan[FRONT + slot] > 0)
                def _():
                    staged[here, :, columns] = tile[
                        slot, up * BLOCK : (up + 1) * BLOCK, :
                    ].astype(jnp.float32)

                @pl.when(plan[FRONT + slot] <= 0)
                def _():
                    staged[here, :, columns] = jnp.zeros((BLOCK, BLOCK), jnp.float32)

            row = pl.multiple_of(block_map[child, row_x * SIDE + z] * BLOCK, BLOCK)
            copy = pltpu.make_async_copy(
                staged.at[here], out.at[pl.ds(row, BLOCK), :], sems.at[here]
            )
            copy.start()
            copies.append(copy)
    for copy in copies:
        copy.wait()


def place_tiles(block_map, plan, parent_rows, tiles):
    blocks = sum(len(chunk) for chunk, _ in tiles)
    return pl.pallas_call(
        functools.partial(place_kernel, list(tiles)),
        out_shape=PARENT,
        in_specs=[SMEM_SPEC] * 2 + [VMEM_SPEC] * len(tiles) + [HELD],
        out_specs=HELD,
        scratch_shapes=[
            pltpu.VMEM((blocks, BLOCK, SLOTS * BLOCK), jnp.float32),
            pltpu.SemaphoreType.DMA((blocks,)),
        ],
        input_output_aliases={2 + len(tiles): 0},
        compiler_params=pltpu.CompilerParams(vmem_limit_bytes=6 * MIB),
        cost_estimate=pl.CostEstimate(flops=0, bytes_accessed=MIB, transcendentals=0),
        name="place",
    )(block_map, plan, *tiles.values(), parent_rows)


def per_device(inv_factors, panel_rows, border, tail, front_sizes, block_map, block_owner):
    inverses, panel = inv_factors[0].reshape(2 * ROWS, PANEL), panel_rows[0]
    left, right = shift(inverses, "x", 1), shift(inverses, "x", -1)
    low, high, far = (shift(panel, "z", -step) for step in RING[1:])
    folded, panel, inverses = fold_tail(tail[0], panel, inverses)
    left, right, folded, panel, inverses = lax.optimization_barrier(
        (left, right, folded, panel, inverses)
    )
    far_first = shift(left[:ROWS], "x", 1)
    far_second = shift(right[ROWS:], "x", -1)

    chunks = lower_chunks(inverses, left, right, far_first, far_second)
    chunks, update, plan = spread(chunks, "z", *blank_rows(block_map, block_owner))
    up, down = make_messages(folded, (panel, low, high, far))
    from_left, from_right = shift(up, "x", 1), shift(down, "x", -1)
    ahead = shift(from_left[ON_AT:], "x", 1)
    behind = shift(from_right[ON_AT:], "x", -1)
    panels = (down, from_left, from_right, ahead, behind)
    link_local, factor_local = eliminate(border[0], chunks, panels)

    rows_x, rows_z = bundle_of(factor_local, "x"), bundle_of(factor_local, "z")
    rows_x, rows_z = lax.optimization_barrier((rows_x, rows_z))
    factor_local = rows_z[:BLOCK]
    tails = (folded, from_left, from_right, ahead, behind)

    tiles = {}
    for chunk in CHUNKS_OF_ROWS:
        rows = make_tile(chunk, front_sizes, rows_x, rows_z, tails)
        there = to_parent(rows)
        if chunk is FIRST:
            there, factor_local = lax.optimization_barrier((there, factor_local))
        gather = direct_bundle if chunk is FIRST else bundle_of
        packed = pack_tiles(plan, gather(there, "x"))
        for step in range(SIDE):
            tile = packed[step * SLOTS : (step + 1) * SLOTS]
            tiles[chunk, step] = shift(tile, "z", step) if step else tile
    for group in GROUPS:
        update = place_tiles(block_map, plan, update, {key: tiles[key] for key in group})
    return link_local[None], factor_local[None], update[None]


def solution(mesh):
    return jax.shard_map(
        per_device,
        mesh=mesh,
        in_specs=(
            P("leaf", None, "front", None),
            P("leaf", "front", None),
            P("leaf", "front", None),
            P("leaf", "front", None),
            P(),
            P(),
            P(),
        ),
        out_specs=(P("leaf", "front", None), P("leaf", "front", None), P("leaf", None, "front")),
        check_vma=False,
    )
```
